768 devices in a mesh: row: 32 (over z_hi, y, core), col: 24 (over z_lo, x).
Axes of the slice: x: 4, y: 8, z: 12 (z_hi: 2, z_lo: 6; z = z_hi * 6 + z_lo), core: 2. Of those that a mesh axis runs over, the one named last changes fastest.
Arguments:
- amplitudes: bfloat16 [36864, 256], P(('row', 'col')), may hold values from -6 to 6
- residual_in: float32 [36864, 256], P(('row', 'col')), may hold values from -6 to 6
- v_tiles: bfloat16 [32, 24, 385, 2304], P('row', 'col'), as said below
- tile_map: int32 [32, 24, 385, 2], P('row', 'col'), may hold values from 0 to 767, as said below
Outputs:
- residual_out: float32 [36864, 256], P(('row', 'col'))
The draws below stay inside these ranges and needn't reach their ends.
Inputs may be any that keep to these rules, and one draw needn't show every extreme that they name: `tile_map`: slot k of device (r, c) names tile row I = r * 24 + i and tile column J = j * 24 + c with 0 <= i < 24, 0 <= j < 32. Slot 0 is the diagonal tile I = J = r * 24 + c. Over all devices each unordered pair of distinct tiles is named in exactly one slot. Slots past a device's stored tiles repeat its diagonal tile; some devices use all 385 slots. `v_tiles`: slot 0 of every device is a symmetric tile; slots that repeat the diagonal tile past the first are zero.
All inputs are finite; a program needn't handle non-finite values.
Results may differ from the reference program's by a relative error of at most 0.0003.
Values may be sent and summed in bfloat16 or wider, within the bound.
No kernel may reach another device: no remote copies, remote signals or barrier semaphores. Data moves between devices by JAX's collectives and lax.ppermute only.
A program may use at most 64 MiB of HBM per device.

```python
import jax
import jax.numpy as jnp
from jax import lax

TILE = 48
P_SIZE = 256
GRID_ROWS = 32
GRID_COLS = 24
KT = 385
M = 36864


def layout_info(key):
    count = GRID_ROWS * GRID_COLS
    slots = count // 2 + 1
    ranks = jax.random.permutation(key, count).astype(jnp.int32)
    device = jnp.arange(count, dtype=jnp.int32)[:, None]
    place = jnp.arange(count, dtype=jnp.int32)[None, :]
    dev_row = device // GRID_COLS
    dev_col = device % GRID_COLS
    pos_i = place // GRID_ROWS
    pos_j = place % GRID_ROWS
    partner = pos_j * GRID_COLS + pos_i
    mine = ranks[device]
    theirs = ranks[partner]
    differ = (theirs - mine) % count
    half = count // 2
    stored = (differ >= 1) & (differ <= half - 1) | (differ == half) & (mine < theirs)
    diagonal = partner == device
    score = jnp.where(diagonal, -1, jnp.where(stored, place, count + place))
    order = jnp.argsort(score, axis=1, stable=True)[:, :slots].astype(jnp.int32)
    live = jnp.take_along_axis(stored | diagonal, order, axis=1)
    sel_i = order // GRID_ROWS
    sel_j = order % GRID_ROWS
    home = dev_row * GRID_COLS + dev_col
    first = jnp.where(live, dev_row * GRID_COLS + sel_i, home)
    second = jnp.where(live, sel_j * GRID_COLS + dev_col, home)
    return (first, second, live)


def draw_tile_map(key, part):
    first, second, live = layout_info(key)
    slots = GRID_ROWS * GRID_COLS // 2 + 1
    table = jnp.stack([first, second], axis=-1)
    return table.reshape(GRID_ROWS, GRID_COLS, slots, 2).astype(jnp.int32)


def draw_v_tiles(key, part):
    first, second, live = layout_info(key)
    key = jax.random.fold_in(key, 23)
    count = GRID_ROWS * GRID_COLS
    slots = count // 2 + 1
    shape = (count, slots, TILE, TILE)
    scale = (TILE * count) ** (-0.5)
    values = jax.random.normal(key, shape, jnp.float32)
    sym = (values + jnp.swapaxes(values, 2, 3)) * 0.70710678
    is_first = (jnp.arange(slots) == 0)[None, :, None, None]
    values = jnp.where(is_first, sym, values)
    values = values * live.astype(jnp.float32)[:, :, None, None] * scale
    return values.reshape(GRID_ROWS, GRID_COLS, slots, TILE * TILE).astype(jnp.bfloat16)


def block_scale(rng, dims, split, smallest, top_value):
    loudness = 1.0
    for dim, parts in split:
        steps = jax.random.uniform(jax.random.fold_in(jax.random.fold_in(rng, 6), dim), (parts,), jnp.float32, smallest / len(split), top_value / len(split))
        loudness = loudness * jnp.repeat(jnp.exp(steps), dims[dim] // parts).reshape((-1,) + (1,) * (len(dims) - 1 - dim))
    return loudness


def bell_draw(key, dims, scale, most, split=(), kind=jnp.bfloat16):
    values = scale * jax.random.normal(key, dims, jnp.float32)
    if split:
        values = values * block_scale(key, dims, split, -0.22, 0.18)
    return jnp.clip(values, -most, most).astype(kind)


def setup_inputs(seed: int = 0) -> dict:
    splits = jax.random.split(jax.random.key(seed), 5)
    return {
        "amplitudes": bell_draw(splits[0], (M, P_SIZE), 1.0, 6.0, ((0, 768),)),
        "residual_in": bell_draw(splits[1], (M, P_SIZE), 1.0, 6.0, ((0, 768),), jnp.float32),
        "v_tiles": draw_v_tiles(jax.random.fold_in(splits[4], 71), 0),
        "tile_map": draw_tile_map(jax.random.fold_in(splits[4], 71), 0),
    }


def reference(amplitudes, residual_in, v_tiles, tile_map):
    ntiles = GRID_ROWS * GRID_COLS
    blocks = amplitudes.astype(jnp.float32).reshape(ntiles, TILE, P_SIZE)
    tiles = v_tiles.reshape(ntiles, KT, TILE, TILE)
    maps = tile_map.reshape(ntiles, KT, 2).astype(jnp.int32)

    def step(total, item):
        weights, entries = item
        wfloat = weights.astype(jnp.float32)
        first = entries[:, 0]
        second = entries[:, 1]
        direct = jnp.einsum("kst,ktp->ksp", wfloat, blocks[second], precision=lax.Precision.HIGHEST)
        mirror = jnp.einsum("kts,ktp->ksp", wfloat, blocks[first], precision=lax.Precision.HIGHEST)
        mirror = mirror * (first != second).astype(jnp.float32)[:, None, None]
        total = total.at[first].add(direct).at[second].add(mirror)
        return total, None

    start = jnp.zeros((ntiles, TILE, P_SIZE), jnp.float32)
    total, unused = lax.scan(step, start, (tiles, maps))
    return residual_in + total.reshape(ntiles * TILE, P_SIZE)
```

```python
import jax
import jax.numpy as jnp
from jax import lax
from jax.experimental import pallas as pl
from jax.experimental.pallas import tpu as pltpu
from jax.sharding import Mesh, PartitionSpec as P

AXES = ("zh", "y", "co", "zl", "x")
SIZES = (2, 8, 2, 6, 4)
ROW_AXES = ("zh", "y", "co")
COL_AXES = ("zl", "x")
TILE = 48
PAIRS = 256
NCOLS = 24
NROWS = 32
PAD = 32
HALF = NROWS * TILE // 2
WIDE = NROWS * TILE
TALL = PAD * TILE
GROUP = 8
LANES = GROUP * TILE


def place_kernel(map_ref, v_ref, x_ref, onehot, dense):
    slots = v_ref.shape[0]
    places = NROWS * PAD

    @pl.when(pl.program_id(0) == 0)
    def _():
        my_zh, my_y, my_co = (lax.axis_index(a) for a in ROW_AXES)
        my_row = my_zh * 16 + my_y * 2 + my_co
        first = map_ref[0:1, :]
        second = map_ref[1:2, :]
        i = first - my_row * NCOLS
        j = (second * 2731) >> 16
        i_place = (i & 3) * 6 + (i >> 2)
        j_place = ((j & 1) ^ my_co) * 16 + ((j >> 1) & 7) * 2 + ((j >> 4) ^ my_zh)
        place = j_place * PAD + i_place
        weight = jnp.where(first == second, 0.5, 1.0)
        for start in range(0, places, 128):
            rows = lax.broadcasted_iota(jnp.int32, (128, slots), 0) + start
            onehot[start : start + 128, :] = jnp.where(rows == place, weight, 0.0).astype(
                jnp.bfloat16
            )

    for start in range(0, places, 256):
        dense[start : start + 256, :] = jnp.dot(
            onehot[start : start + 256, :], v_ref[...], preferred_element_type=jnp.float32
        ).astype(jnp.bfloat16)
    for s in range(GROUP):
        parts = [
            dense[j * PAD : (j + 1) * PAD, s * TILE : (s + 1) * TILE] for j in range(NROWS)
        ]
        x_ref[s * PAD : (s + 1) * PAD, :] = jnp.concatenate(parts, axis=1)


def place(tile_map, v_tiles):
    slots = v_tiles.shape[0]
    return pl.pallas_call(
        place_kernel,
        grid=(TILE // GROUP,),
        in_specs=[
            pl.BlockSpec((2, slots), lambda g: (0, 0)),
            pl.BlockSpec((slots, LANES), lambda g: (0, g)),
        ],
        out_specs=pl.BlockSpec((GROUP * PAD, WIDE), lambda g: (g, 0)),
        out_shape=jax.ShapeDtypeStruct((TALL, WIDE), jnp.bfloat16),
        scratch_shapes=[
            pltpu.VMEM((NROWS * PAD, slots), jnp.bfloat16),
            pltpu.VMEM((NROWS * PAD, LANES), jnp.bfloat16),
        ],
        compiler_params=pltpu.CompilerParams(vmem_limit_bytes=32 * 2**20),
        cost_estimate=pl.CostEstimate(
            flops=2 * 1024 * 512 * 2304, bytes_accessed=8 * 2**20, transcendentals=0
        ),
        name="place",
    )(tile_map, v_tiles)


def mirror_kernel(x_ref, a_ref, own_ref, other_ref, left, right, rows):
    wides = (left, right)
    for h, wide in enumerate(wides):
        lanes = slice(h * 128, h * 128 + 128)
        for i in range(NCOLS):
            wide[pl.ds(i, TILE, stride=PAD), :] = a_ref[i, :, lanes].astype(jnp.float32)
        for i in range(NCOLS, PAD):
            wide[pl.ds(i, TILE, stride=PAD), :] = jnp.zeros((TILE, 128), jnp.float32)
        rows[:, lanes] = wide[...].astype(jnp.bfloat16)
    for out, base in ((other_ref, HALF), (own_ref, 0)):
        for start in range(0, HALF, 256):
            out[start : start + 256, :] = lax.dot_general(
                x_ref[:, base + start : base + start + 256],
                rows[...],
                (((0,), (0,)), ((), ())),
                preferred_element_type=jnp.float32,
            )


def mirror(x, a):
    half = jax.ShapeDtypeStruct((HALF, PAIRS), jnp.float32)
    return pl.pallas_call(
        mirror_kernel,
        out_shape=(half, half),
        scratch_shapes=[
            pltpu.VMEM((TALL, 128), jnp.float32),
            pltpu.VMEM((TALL, 128), jnp.float32),
            pltpu.VMEM((TALL, PAIRS), jnp.bfloat16),
        ],
        compiler_params=pltpu.CompilerParams(vmem_limit_bytes=32 * 2**20),
        cost_estimate=pl.CostEstimate(
            flops=2 * TALL * WIDE * PAIRS, bytes_accessed=8 * 2**20, transcendentals=0
        ),
        name="mirror",
    )(x, a)


def direct_kernel(x_ref, own_ref, other_ref, out_ref, left, right):
    for start in range(0, TALL, 256):
        total = jnp.dot(
            x_ref[start : start + 256, :HALF], own_ref[...], preferred_element_type=jnp.float32
        ) + jnp.dot(
            x_ref[start : start + 256, HALF:], other_ref[...], preferred_element_type=jnp.float32
        )
        left[start : start + 256, :] = total[:, :128]
        right[start : start + 256, :] = total[:, 128:]
    for i in range(NCOLS):
        out_ref[i, :, :128] = left[pl.ds(i, TILE, stride=PAD), :]
        out_ref[i, :, 128:] = right[pl.ds(i, TILE, stride=PAD), :]


def direct(x, own, other):
    return pl.pallas_call(
        direct_kernel,
        out_shape=jax.ShapeDtypeStruct((NCOLS, TILE, PAIRS), jnp.float32),
        scratch_shapes=[
            pltpu.VMEM((TALL, 128), jnp.float32),
            pltpu.VMEM((TALL, 128), jnp.float32),
        ],
        compiler_params=pltpu.CompilerParams(vmem_limit_bytes=32 * 2**20),
        cost_estimate=pl.CostEstimate(
            flops=2 * TALL * WIDE * PAIRS, bytes_accessed=8 * 2**20, transcendentals=0
        ),
        name="direct",
    )(x, own, other)


SWAP = [(0, 1), (1, 0)]


def spread(block, axis, count):
    copies = jnp.broadcast_to(block[None], (count,) + block.shape)
    return lax.all_to_all(copies, axis, split_axis=0, concat_axis=0)


def per_device(amplitudes, residual_in, v_tiles, tile_map):
    far = lax.ppermute(amplitudes, "zh", SWAP)
    line = spread(amplitudes, "zl", 6)
    pair = jnp.stack([amplitudes, far])
    own = spread(pair, "y", 8).reshape(HALF, PAIRS)
    rows = spread(line, "x", 4).reshape(NCOLS, TILE, PAIRS)
    other = lax.ppermute(own, "co", SWAP)
    x = place(tile_map[0, 0].T, v_tiles[0, 0])

    keep, send = mirror(x, rows)
    got = lax.ppermute(send, "co", SWAP)
    ladder_rows = direct(x, own, other)
    col_parts = lax.all_to_all(
        ladder_rows.reshape(4, 6 * TILE, PAIRS), "x", split_axis=0, concat_axis=0
    )
    row_parts = lax.all_to_all(
        (keep + got).reshape(8, 2 * TILE, PAIRS), "y", split_axis=0, concat_axis=0
    )
    col_line = jnp.sum(col_parts, axis=0).reshape(6, TILE, PAIRS)
    col_line = lax.all_to_all(col_line, "zl", split_axis=0, concat_axis=0)
    row_pair = jnp.sum(row_parts, axis=0).reshape(2, TILE, PAIRS)
    row_far = lax.ppermute(row_pair[1], "zh", SWAP)
    return residual_in + row_pair[0] + jnp.sum(col_line, axis=0) + row_far


def solution(mesh):
    fine = Mesh(mesh.devices.reshape(SIZES), AXES)
    return jax.shard_map(
        per_device,
        mesh=fine,
        in_specs=(
            P(AXES, None),
            P(AXES, None),
            P(ROW_AXES, COL_AXES, None, None),
            P(ROW_AXES, COL_AXES, None, None),
        ),
        out_specs=P(AXES, None),
        check_vma=False,
    )
```

```python
import jax
import jax.numpy as jnp
from jax import lax
from jax.experimental import pallas as pl
from jax.experimental.pallas import tpu as pltpu
from jax.sharding import Mesh, PartitionSpec as P

AXES = ("zh", "y", "co", "zl", "x")
SIZES = (2, 8, 2, 6, 4)
ROW_AXES = ("zh", "y", "co")
COL_AXES = ("zl", "x")
TILE = 48
PAIRS = 256
NCOLS = 24
NROWS = 32
PAD = 32
HALF = NROWS * TILE // 2
WIDE = NROWS * TILE
TALL = PAD * TILE
GROUP = 8
LANES = GROUP * TILE


def place_kernel(map_ref, v_ref, x_ref, token_ref, onehot, dense):
    slots = v_ref.shape[0]
    places = NROWS * PAD

    @pl.when(pl.program_id(0) == 0)
    def _():
        token_ref[...] = jnp.zeros_like(token_ref)
        my_zh, my_y, my_co = (lax.axis_index(a) for a in ROW_AXES)
        my_zl, my_x = (lax.axis_index(a) for a in COL_AXES)
        my_row = my_zh * 16 + my_y * 2 + my_co
        first = map_ref[0:1, :]
        second = map_ref[1:2, :]
        i = first - my_row * NCOLS
        j = (second * 2731) >> 16
        run = (i >> 3) - (my_zl >> 1)
        run = jnp.where(run < 0, run + 3, run)
        i_place = ((i & 3) ^ my_x) * 6 + run * 2 + (((i >> 2) & 1) ^ (my_zl & 1))
        j_place = ((j & 1) ^ my_co) * 16 + ((j >> 1) & 7) * 2 + ((j >> 4) ^ my_zh)
        place = j_place * PAD + i_place
        weight = jnp.where(first == second, 0.5, 1.0)
        for start in range(0, places, 128):
            rows = lax.broadcasted_iota(jnp.int32, (128, slots), 0) + start
            onehot[start : start + 128, :] = jnp.where(rows == place, weight, 0.0).astype(
                jnp.bfloat16
            )

    for start in range(0, places, 256):
        dense[start : start + 256, :] = jnp.dot(
            onehot[start : start + 256, :], v_ref[...], preferred_element_type=jnp.float32
        ).astype(jnp.bfloat16)
    for s in range(GROUP):
        parts = [
            dense[j * PAD : (j + 1) * PAD, s * TILE : (s + 1) * TILE] for j in range(NROWS)
        ]
        x_ref[s * PAD : (s + 1) * PAD, :] = jnp.concatenate(parts, axis=1)


def place(tile_map, v_tiles):
    slots = v_tiles.shape[0]
    return pl.pallas_call(
        place_kernel,
        grid=(TILE // GROUP,),
        in_specs=[
            pl.BlockSpec((2, slots), lambda g: (0, 0)),
            pl.BlockSpec((slots, LANES), lambda g: (0, g)),
        ],
        out_specs=(
            pl.BlockSpec((GROUP * PAD, WIDE), lambda g: (g, 0)),
            pl.BlockSpec((8, 128), lambda g: (0, 0)),
        ),
        out_shape=(
            jax.ShapeDtypeStruct((TALL, WIDE), jnp.bfloat16),
            jax.ShapeDtypeStruct((8, 128), jnp.float32),
        ),
        scratch_shapes=[
            pltpu.VMEM((NROWS * PAD, slots), jnp.bfloat16),
            pltpu.VMEM((NROWS * PAD, LANES), jnp.bfloat16),
        ],
        compiler_params=pltpu.CompilerParams(vmem_limit_bytes=8 * 2**20),
        cost_estimate=pl.CostEstimate(
            flops=2 * 1024 * 512 * 2304, bytes_accessed=8 * 2**20, transcendentals=0
        ),
        name="place",
    )(tile_map, v_tiles)


def mirror_kernel(after, x_ref, a0, a1, a2, a3, own_ref, other_ref, left, right, rows):
    wides = (left, right)
    blocks = [a.at[pl.ds(k * TILE, TILE), :] for a in (a0, a1, a2, a3) for k in range(6)]
    for h, wide in enumerate(wides):
        lanes = slice(h * 128, h * 128 + 128)
        for i in range(NCOLS):
            wide[pl.ds(i, TILE, stride=PAD), :] = blocks[i][:, lanes].astype(jnp.float32)
        for i in range(NCOLS, PAD):
            wide[pl.ds(i, TILE, stride=PAD), :] = jnp.zeros((TILE, 128), jnp.float32)
        rows[:, lanes] = wide[...].astype(jnp.bfloat16)
    for out, base in ((other_ref, HALF), (own_ref, 0)):
        for start in range(0, HALF, 256):
            out[start : start + 256, :] = lax.dot_general(
                x_ref[:, base + start : base + start + 256],
                rows[...],
                (((0,), (0,)), ((), ())),
                preferred_element_type=jnp.float32,
            )


def mirror(after, x, *quarters):
    half = jax.ShapeDtypeStruct((HALF, PAIRS), jnp.float32)
    return pl.pallas_call(
        mirror_kernel,
        in_specs=[pl.BlockSpec(memory_space=pl.ANY)]
        + [pl.BlockSpec(memory_space=pltpu.VMEM)] * 5,
        out_shape=(half, half),
        scratch_shapes=[
            pltpu.VMEM((TALL, 128), jnp.float32),
            pltpu.VMEM((TALL, 128), jnp.float32),
            pltpu.VMEM((TALL, PAIRS), jnp.bfloat16),
        ],
        compiler_params=pltpu.CompilerParams(vmem_limit_bytes=16 * 2**20),
        cost_estimate=pl.CostEstimate(
            flops=2 * TALL * WIDE * PAIRS, bytes_accessed=8 * 2**20, transcendentals=0
        ),
        name="mirror",
    )(after, x, *quarters)


def direct_kernel(x_ref, own_ref, other_ref, o0, o1, o2, o3, left, right):
    for start in range(0, TALL, 256):
        total = jnp.dot(
            x_ref[start : start + 256, :HALF], own_ref[...], preferred_element_type=jnp.float32
        ) + jnp.dot(
            x_ref[start : start + 256, HALF:], other_ref[...], preferred_element_type=jnp.float32
        )
        left[start : start + 256, :] = total[:, :128]
        right[start : start + 256, :] = total[:, 128:]
    for i in range(NCOLS):
        out = (o0, o1, o2, o3)[i // 6]
        rows = slice(i % 6 * TILE, i % 6 * TILE + TILE)
        out[rows, :128] = left[pl.ds(i, TILE, stride=PAD), :]
        out[rows, 128:] = right[pl.ds(i, TILE, stride=PAD), :]


def direct(x, own, other):
    return pl.pallas_call(
        direct_kernel,
        out_shape=(jax.ShapeDtypeStruct((6 * TILE, PAIRS), jnp.float32),) * 4,
        scratch_shapes=[
            pltpu.VMEM((TALL, 128), jnp.float32),
            pltpu.VMEM((TALL, 128), jnp.float32),
        ],
        compiler_params=pltpu.CompilerParams(vmem_limit_bytes=16 * 2**20),
        cost_estimate=pl.CostEstimate(
            flops=2 * TALL * WIDE * PAIRS, bytes_accessed=8 * 2**20, transcendentals=0
        ),
        name="direct",
    )(x, own, other)


def stack_kernel(*refs):
    *blocks, out = refs
    start = 0
    for block in blocks:
        out[start : start + block.shape[0], :] = block[...]
        start += block.shape[0]


def stack(*blocks):
    rows = sum(b.shape[0] for b in blocks)
    return pl.pallas_call(
        stack_kernel,
        out_shape=jax.ShapeDtypeStruct((rows, PAIRS), blocks[0].dtype),
        compiler_params=pltpu.CompilerParams(vmem_limit_bytes=4 * 2**20),
        name="stack",
    )(*blocks)


def begin_kernel(after, own, far, beside, pair, both):
    pair[:TILE, :] = own[...]
    pair[TILE:, :] = beside[...]
    for n in range(8):
        both[n, :TILE, :] = own[...]
        both[n, TILE:, :] = far[...]


def begin(after, own, far, beside):
    return pl.pallas_call(
        begin_kernel,
        in_specs=[pl.BlockSpec(memory_space=pl.ANY)]
        + [pl.BlockSpec(memory_space=pltpu.VMEM)] * 3,
        out_shape=(
            jax.ShapeDtypeStruct((2 * TILE, PAIRS), own.dtype),
            jax.ShapeDtypeStruct((8, 2 * TILE, PAIRS), own.dtype),
        ),
        compiler_params=pltpu.CompilerParams(vmem_limit_bytes=4 * 2**20),
        name="begin",
    )(after, own, far, beside)


def total_kernel(count, *refs):
    parts = refs[:count]
    outs = refs[count:]
    rows = outs[0].shape[0]
    for k, out in enumerate(outs):
        terms = []
        for p in parts:
            if len(p.shape) == 3:
                terms += [p[n, k * rows : (k + 1) * rows, :] for n in range(p.shape[0])]
            else:
                terms.append(p[k * rows : (k + 1) * rows, :])
        while len(terms) > 1:
            terms = [sum(terms[n : n + 2]) for n in range(0, len(terms), 2)]
        out[...] = terms[0]


def total(splits, *parts):
    rows = parts[0].shape[-2] // splits
    return pl.pallas_call(
        lambda *refs: total_kernel(len(parts), *refs),
        out_shape=(jax.ShapeDtypeStruct((rows, PAIRS), jnp.float32),) * splits,
        compiler_params=pltpu.CompilerParams(vmem_limit_bytes=8 * 2**20),
        name="total",
    )(*parts)


SWAP = [(0, 1), (1, 0)]


def swap_x(block, k):
    return lax.ppermute(block, "x", [(i, i ^ k) for i in range(4)])


def swap_zl(block):
    return lax.ppermute(block, "zl", [(i, i ^ 1) for i in range(6)])


def turn_zl(block, k):
    return lax.ppermute(block, "zl", [(i, (i + 2 * k) % 6) for i in range(6)])


def per_device(amplitudes, residual_in, v_tiles, tile_map):
    far = lax.ppermute(amplitudes, "zh", SWAP)
    beside = swap_zl(amplitudes)
    x, placed = place(tile_map[0, 0].T, v_tiles[0, 0])

    pair, both = begin(placed, amplitudes, far, beside)
    line = stack(pair, turn_zl(pair, 2), turn_zl(pair, 1))
    quarters = [line] + [swap_x(line, k) for k in (1, 2, 3)]

    own = lax.all_to_all(both, "y", split_axis=0, concat_axis=0).reshape(HALF, PAIRS)
    other = lax.ppermute(own, "co", SWAP)

    keep, send = mirror(own, x, *quarters)
    got = lax.ppermute(send, "co", SWAP)
    row_parts = lax.all_to_all(
        total(1, keep, got)[0].reshape(8, 2 * TILE, PAIRS), "y", split_axis=0, concat_axis=0
    )

    parts = direct(x, own, other)
    run0, run1, run2 = total(3, parts[0], *(swap_x(parts[k], k) for k in (1, 2, 3)))
    col_near, col_send = total(2, run0, turn_zl(run1, 1), turn_zl(run2, 2))
    col_beside = swap_zl(col_send)

    row_near, row_send = total(2, row_parts)
    row_far = lax.ppermute(row_send, "zh", SWAP)
    return residual_in + row_near + col_near + col_beside + row_far


def solution(mesh):
    fine = Mesh(mesh.devices.reshape(SIZES), AXES)
    return jax.shard_map(
        per_device,
        mesh=fine,
        in_specs=(
            P(AXES, None),
            P(AXES, None),
            P(ROW_AXES, COL_AXES, None, None),
            P(ROW_AXES, COL_AXES, None, None),
        ),
        out_specs=P(AXES, None),
        check_vma=False,
    )
```

```python
import jax
import jax.numpy as jnp
from jax import lax
from jax.experimental import pallas as pl
from jax.experimental.pallas import tpu as pltpu
from jax.sharding import Mesh, PartitionSpec as P

AXES = ("zh", "y", "co", "zl", "x")
SIZES = (2, 8, 2, 6, 4)
ROW_AXES = ("zh", "y", "co")
COL_AXES = ("zl", "x")
TILE = 48
PAIRS = 256
NCOLS = 24
NROWS = 32
PAD = 32
HALF = NROWS * TILE // 2
WIDE = NROWS * TILE
TALL = PAD * TILE
GROUP = 8
GROUPS = TILE // GROUP
LANES = GROUP * TILE
CHUNK = 256
CHUNKS = WIDE // CHUNK
LINE = 6 * TILE
EXTRA = 16
HBM = pl.BlockSpec(memory_space=pltpu.HBM)
VMEM = pl.BlockSpec(memory_space=pltpu.VMEM)


def params(mib):
    return pltpu.CompilerParams(vmem_limit_bytes=mib * 2**20)


def place_kernel(map_ref, v_hbm, x_hbm, token_ref, v, x, onehot, dense, v_sem, x_sem):
    slots = v_hbm.shape[0]
    places = NROWS * PAD

    def v_copy(g):
        lanes = pl.ds(pl.multiple_of(g * LANES, LANES), LANES)
        return pltpu.make_async_copy(v_hbm.at[:, lanes], v.at[g], v_sem.at[g])

    def x_copy(g):
        rows = pl.ds(pl.multiple_of(g * CHUNK, CHUNK), CHUNK)
        return pltpu.make_async_copy(x.at[rows, :], x_hbm.at[rows, :], x_sem.at[g])

    for g in range(GROUPS):
        v_copy(g).start()
    token_ref[...] = jnp.zeros_like(token_ref)
    my_zh, my_y, my_co = (lax.axis_index(a) for a in ROW_AXES)
    my_x = lax.axis_index("x")
    my_row = my_zh * 16 + my_y * 2 + my_co
    first = map_ref[0:1, :]
    second = map_ref[1:2, :]
    i = first - my_row * NCOLS
    j = (second * 2731) >> 16
    i_place = ((i & 3) ^ my_x) * 6 + (i >> 2)
    j_place = ((j & 1) ^ my_co) * 16 + ((j >> 1) & 7) * 2 + ((j >> 4) ^ my_zh)
    place = j_place * PAD + i_place
    weight = jnp.where(first == second, 0.5, 1.0)
    for start in range(0, places, 128):
        rows = lax.broadcasted_iota(jnp.int32, (128, slots), 0) + start
        onehot[start : start + 128, :] = jnp.where(rows == place, weight, 0.0).astype(
            jnp.bfloat16
        )

    @pl.loop(0, GROUPS)
    def _(g):
        v_copy(g).wait()
        for start in range(0, places, 256):
            dense[start : start + 256, :] = jnp.dot(
                onehot[start : start + 256, :], v[g], preferred_element_type=jnp.float32
            ).astype(jnp.bfloat16)
        for s in range(GROUP):
            parts = [
                dense[j * PAD : (j + 1) * PAD, s * TILE : (s + 1) * TILE] for j in range(NROWS)
            ]
            rows = pl.ds(pl.multiple_of(g * CHUNK + s * PAD, PAD), PAD)
            x[rows, :] = jnp.concatenate(parts, axis=1)
        x_copy(g).start()

    for g in range(GROUPS):
        x_copy(g).wait()


def place(tile_map, v_tiles):
    slots = v_tiles.shape[0]
    return pl.pallas_call(
        place_kernel,
        in_specs=[VMEM, HBM],
        out_specs=(HBM, VMEM),
        out_shape=(
            jax.ShapeDtypeStruct((TALL, WIDE), jnp.bfloat16),
            jax.ShapeDtypeStruct((8, 128), jnp.float32),
        ),
        scratch_shapes=[
            pltpu.VMEM((GROUPS, slots, LANES), jnp.bfloat16),
            pltpu.VMEM((TALL, WIDE), jnp.bfloat16),
            pltpu.VMEM((NROWS * PAD, slots), jnp.bfloat16),
            pltpu.VMEM((NROWS * PAD, LANES), jnp.bfloat16),
            pltpu.SemaphoreType.DMA((GROUPS,)),
            pltpu.SemaphoreType.DMA((GROUPS,)),
        ],
        compiler_params=params(60),
        cost_estimate=pl.CostEstimate(
            flops=2 * 1024 * 512 * 2304, bytes_accessed=8 * 2**20, transcendentals=0
        ),
        name="place",
    )(tile_map, v_tiles)


def begin_kernel(after, own, far, both):
    for n in range(8):
        both[n, :TILE, :] = own[...]
        both[n, TILE:, :] = far[...]


def begin(after, own, far):
    return pl.pallas_call(
        begin_kernel,
        in_specs=[pl.BlockSpec(memory_space=pl.ANY), VMEM, VMEM],
        out_shape=jax.ShapeDtypeStruct((8, 2 * TILE, PAIRS), own.dtype),
        compiler_params=params(4),
        name="begin",
    )(after, own, far)


def mirror_kernel(after, x_hbm, a0, a1, a2, a3, own_ref, other_ref, x, left, right, rows, sem):
    def copy(c):
        return pltpu.make_async_copy(
            x_hbm.at[:, c * CHUNK : (c + 1) * CHUNK], x.at[c], sem.at[c]
        )

    order = (3, 4, 5, 0, 1, 2)
    for c in order:
        copy(c).start()
    blocks = [a.at[k] for a in (a0, a1, a2, a3) for k in range(6)]
    for h, wide in enumerate((left, right)):
        lanes = slice(h * 128, h * 128 + 128)
        for i in range(NCOLS):
            wide[pl.ds(i, TILE, stride=PAD), :] = blocks[i][:, lanes].astype(jnp.float32)
        for i in range(NCOLS, PAD):
            wide[pl.ds(i, TILE, stride=PAD), :] = jnp.zeros((TILE, 128), jnp.float32)
        rows[:, lanes] = wide[...].astype(jnp.bfloat16)
    for c in order:
        copy(c).wait()
        out = own_ref if c < 3 else other_ref
        start = c % 3 * CHUNK
        out[start : start + CHUNK, :] = lax.dot_general(
            x[c], rows[...], (((0,), (0,)), ((), ())), preferred_element_type=jnp.float32
        )


def mirror(after, x, *quarters):
    half = jax.ShapeDtypeStruct((HALF, PAIRS), jnp.float32)
    return pl.pallas_call(
        mirror_kernel,
        in_specs=[pl.BlockSpec(memory_space=pl.ANY), HBM] + [VMEM] * 4,
        out_shape=(half, half),
        scratch_shapes=[
            pltpu.VMEM((CHUNKS, TALL, CHUNK), jnp.bfloat16),
            pltpu.VMEM((TALL, 128), jnp.float32),
            pltpu.VMEM((TALL, 128), jnp.float32),
            pltpu.VMEM((TALL, PAIRS), jnp.bfloat16),
            pltpu.SemaphoreType.DMA((CHUNKS,)),
        ],
        compiler_params=params(60),
        cost_estimate=pl.CostEstimate(
            flops=2 * TALL * WIDE * PAIRS, bytes_accessed=8 * 2**20, transcendentals=0
        ),
        name="mirror",
    )(after, x, *quarters)


def code(groups, out):
    row = lax.broadcasted_iota(jnp.int32, (EXTRA, PAIRS), 0)
    extra = jnp.zeros((EXTRA, PAIRS), jnp.int32)
    for n, block in enumerate(groups):
        top = jnp.max(jnp.abs(block), axis=0, keepdims=True)
        power = jnp.ceil(jnp.log2(jnp.maximum(top, 2.0**-100)))
        scaled = jnp.floor(block * jnp.exp2(15.0 - power) + 0.5)
        whole = jnp.clip(scaled, -32767.0, 32767.0).astype(jnp.int32)
        out[n * TILE : (n + 1) * TILE, :] = whole.astype(jnp.int16)
        extra = jnp.where(row == n, power.astype(jnp.int32), extra)
    out[len(groups) * TILE :, :] = extra.astype(jnp.int16)


def decode(coded, count):
    extra = coded[count * TILE :, :].astype(jnp.int32).astype(jnp.float32)
    step = jnp.exp2(extra - 15.0)
    return [
        coded[n * TILE : (n + 1) * TILE, :].astype(jnp.int32).astype(jnp.float32)
        * step[n : n + 1, :]
        for n in range(count)
    ]


def direct_kernel(x_hbm, own_ref, other_ref, o0, o1, o2, o3, x, left, right, sem):
    def copy(c):
        rows = slice(c * CHUNK, (c + 1) * CHUNK)
        return pltpu.make_async_copy(x_hbm.at[rows, :], x.at[rows, :], sem.at[c])

    for c in range(CHUNKS):
        copy(c).start()
    for c in range(CHUNKS):
        rows = slice(c * CHUNK, (c + 1) * CHUNK)
        copy(c).wait()
        both = jnp.dot(
            x[rows, :HALF], own_ref[...], preferred_element_type=jnp.float32
        ) + jnp.dot(x[rows, HALF:], other_ref[...], preferred_element_type=jnp.float32)
        left[rows, :] = both[:, :128]
        right[rows, :] = both[:, 128:]

    def block(i):
        rows = pl.ds(i, TILE, stride=PAD)
        return jnp.concatenate([left[rows, :], right[rows, :]], axis=1)

    for q, out in ((1, o1), (2, o2), (3, o3)):
        code([block(q * 6 + n) for n in range(6)], out)
    for n in range(6):
        o0[n * TILE : (n + 1) * TILE, :] = block(n)


def direct(x, own, other):
    coded = jax.ShapeDtypeStruct((LINE + EXTRA, PAIRS), jnp.int16)
    return pl.pallas_call(
        direct_kernel,
        in_specs=[HBM, VMEM, VMEM],
        out_shape=(jax.ShapeDtypeStruct((LINE, PAIRS), jnp.float32),) + (coded,) * 3,
        scratch_shapes=[
            pltpu.VMEM((TALL, WIDE), jnp.bfloat16),
            pltpu.VMEM((TALL, 128), jnp.float32),
            pltpu.VMEM((TALL, 128), jnp.float32),
            pltpu.SemaphoreType.DMA((CHUNKS,)),
        ],
        compiler_params=params(60),
        cost_estimate=pl.CostEstimate(
            flops=2 * TALL * WIDE * PAIRS, bytes_accessed=8 * 2**20, transcendentals=0
        ),
        name="direct",
    )(x, own, other)


def code_y_kernel(keep, got, out):
    @pl.loop(0, 8)
    def _(n):
        rows = pl.multiple_of(n * 2 * TILE, 2 * TILE)
        groups = [
            keep[pl.ds(rows + k * TILE, TILE), :] + got[pl.ds(rows + k * TILE, TILE), :]
            for k in range(2)
        ]
        code(groups, out.at[n])


def code_y(keep, got):
    return pl.pallas_call(
        code_y_kernel,
        out_shape=jax.ShapeDtypeStruct((8, 2 * TILE + EXTRA, PAIRS), jnp.int16),
        compiler_params=params(6),
        name="code_y",
    )(keep, got)


def sum_y_kernel(coded, near, send):
    totals = decode(coded.at[0], 2)
    for n in range(1, 8):
        totals = [a + b for a, b in zip(totals, decode(coded.at[n], 2))]
    near[...], send[...] = totals


def sum_y(coded):
    return pl.pallas_call(
        sum_y_kernel,
        out_shape=(jax.ShapeDtypeStruct((TILE, PAIRS), jnp.float32),) * 2,
        compiler_params=params(4),
        name="sum_y",
    )(coded)


def sum_x_kernel(keep, c1, c2, c3, out):
    parts = [decode(c, 6) for c in (c1, c2, c3)]
    for n in range(6):
        out[n] = (keep[n * TILE : (n + 1) * TILE, :] + parts[0][n]) + (parts[1][n] + parts[2][n])


def sum_x(keep, *coded):
    return pl.pallas_call(
        sum_x_kernel,
        out_shape=jax.ShapeDtypeStruct((6, TILE, PAIRS), jnp.float32),
        compiler_params=params(4),
        name="sum_x",
    )(keep, *coded)


def end_kernel(residual, near, far, line, out):
    a = (line[0] + line[1]) + (line[2] + line[3])
    out[...] = (residual[...] + (near[...] + far[...])) + (a + (line[4] + line[5]))


def end(residual, near, far, line):
    return pl.pallas_call(
        end_kernel,
        out_shape=jax.ShapeDtypeStruct((TILE, PAIRS), jnp.float32),
        compiler_params=params(4),
        name="end",
    )(residual, near, far, line)


SWAP = [(0, 1), (1, 0)]


def swap_x(block, k):
    return lax.ppermute(block, "x", [(i, i ^ k) for i in range(4)])


def trade(block, axis):
    return lax.all_to_all(block, axis, split_axis=0, concat_axis=0)


def per_device(amplitudes, residual_in, v_tiles, tile_map):
    far = lax.ppermute(amplitudes, "zh", SWAP)
    line = trade(jnp.broadcast_to(amplitudes[None], (6, TILE, PAIRS)), "zl")
    x, placed = place(tile_map[0, 0].T, v_tiles[0, 0])
    own = trade(begin(placed, amplitudes, far), "y").reshape(HALF, PAIRS)
    other = lax.ppermute(own, "co", SWAP)

    keep, send = mirror(own, x, line, *(swap_x(line, k) for k in (1, 2, 3)))
    got = lax.ppermute(send, "co", SWAP)
    row_parts = trade(code_y(keep, got), "y")

    parts = direct(x, own, other)
    col_line = sum_x(parts[0], *(swap_x(parts[k], k) for k in (1, 2, 3)))
    col_line = trade(col_line, "zl")

    row_near, row_send = sum_y(row_parts)
    row_far = lax.ppermute(row_send, "zh", SWAP)
    return end(residual_in, row_near, row_far, col_line)


def solution(mesh):
    fine = Mesh(mesh.devices.reshape(SIZES), AXES)
    return jax.shard_map(
        per_device,
        mesh=fine,
        in_specs=(
            P(AXES, None),
            P(AXES, None),
            P(ROW_AXES, COL_AXES, None, None),
            P(ROW_AXES, COL_AXES, None, None),
        ),
        out_specs=P(AXES, None),
        check_vma=False,
    )
```

```python
import functools

import jax
import jax.numpy as jnp
from jax import lax
from jax.experimental import pallas as pl
from jax.experimental.pallas import tpu as pltpu
from jax.sharding import Mesh, PartitionSpec as P

AXES = ("zh", "y", "co", "zl", "x")
SIZES = (2, 8, 2, 6, 4)
ROW_AXES = ("zh", "y", "co")
COL_AXES = ("zl", "x")
TILE = 48
PAIRS = 256
NCOLS = 24
NROWS = 32
PAD = 32
HALF = NROWS * TILE // 2
WIDE = NROWS * TILE
TALL = PAD * TILE
GROUP = 8
GROUPS = TILE // GROUP
LANES = GROUP * TILE
CHUNK = 256
CHUNKS = WIDE // CHUNK
LINE = 6 * TILE
EXTRA = 16
HBM = pl.BlockSpec(memory_space=pltpu.HBM)
VMEM = pl.BlockSpec(memory_space=pltpu.VMEM)


def params(mib):
    return pltpu.CompilerParams(vmem_limit_bytes=mib * 2**20)


def place_kernel(map_ref, v_hbm, x_hbm, token_ref, v, x, onehot, dense, v_sem, x_sem):
    slots = v_hbm.shape[0]
    places = NROWS * PAD

    def v_copy(g):
        lanes = pl.ds(pl.multiple_of(g * LANES, LANES), LANES)
        return pltpu.make_async_copy(v_hbm.at[:, lanes], v.at[g], v_sem.at[g])

    def x_copy(g):
        rows = pl.ds(pl.multiple_of(g * CHUNK, CHUNK), CHUNK)
        return pltpu.make_async_copy(x.at[rows, :], x_hbm.at[rows, :], x_sem.at[g])

    for g in range(GROUPS):
        v_copy(g).start()
    token_ref[...] = jnp.zeros_like(token_ref)
    my_zh, my_y, my_co = (lax.axis_index(a) for a in ROW_AXES)
    my_x = lax.axis_index("x")
    my_row = my_zh * 16 + my_y * 2 + my_co
    first = map_ref[0:1, :]
    second = map_ref[1:2, :]
    i = first - my_row * NCOLS
    j = (second * 2731) >> 16
    i_place = ((i & 3) ^ my_x) * 6 + (i >> 2)
    j_place = ((j & 1) ^ my_co) * 16 + ((j >> 1) & 7) * 2 + ((j >> 4) ^ my_zh)
    place = j_place * PAD + i_place
    weight = jnp.where(first == second, 0.5, 1.0)
    for start in range(0, places, 128):
        rows = lax.broadcasted_iota(jnp.int32, (128, slots), 0) + start
        onehot[start : start + 128, :] = jnp.where(rows == place, weight, 0.0).astype(
            jnp.bfloat16
        )

    @pl.loop(0, GROUPS)
    def _(g):
        v_copy(g).wait()
        for start in range(0, places, 256):
            dense[start : start + 256, :] = jnp.dot(
                onehot[start : start + 256, :], v[g], preferred_element_type=jnp.float32
            ).astype(jnp.bfloat16)
        for s in range(GROUP):
            parts = [
                dense[j * PAD : (j + 1) * PAD, s * TILE : (s + 1) * TILE] for j in range(NROWS)
            ]
            rows = pl.ds(pl.multiple_of(g * CHUNK + s * PAD, PAD), PAD)
            x[rows, :] = jnp.concatenate(parts, axis=1)
        x_copy(g).start()

    for g in range(GROUPS):
        x_copy(g).wait()


def place(tile_map, v_tiles):
    slots = v_tiles.shape[0]
    return pl.pallas_call(
        place_kernel,
        in_specs=[VMEM, HBM],
        out_specs=(HBM, VMEM),
        out_shape=(
            jax.ShapeDtypeStruct((TALL, WIDE), jnp.bfloat16),
            jax.ShapeDtypeStruct((8, 128), jnp.float32),
        ),
        scratch_shapes=[
            pltpu.VMEM((GROUPS, slots, LANES), jnp.bfloat16),
            pltpu.VMEM((TALL, WIDE), jnp.bfloat16),
            pltpu.VMEM((NROWS * PAD, slots), jnp.bfloat16),
            pltpu.VMEM((NROWS * PAD, LANES), jnp.bfloat16),
            pltpu.SemaphoreType.DMA((GROUPS,)),
            pltpu.SemaphoreType.DMA((GROUPS,)),
        ],
        compiler_params=params(60),
        cost_estimate=pl.CostEstimate(
            flops=2 * 1024 * 512 * 2304, bytes_accessed=8 * 2**20, transcendentals=0
        ),
        name="place",
    )(tile_map, v_tiles)


def copies_kernel(skip, *refs):
    *blocks, out = refs[skip:]
    for n in range(out.shape[0]):
        start = 0
        for block in blocks:
            out[n, start : start + block.shape[0], :] = block[...]
            start += block.shape[0]


def copies(count, after, *blocks):
    rows = sum(b.shape[0] for b in blocks)
    return pl.pallas_call(
        functools.partial(copies_kernel, len(after)),
        in_specs=[pl.BlockSpec(memory_space=pl.ANY)] * len(after) + [VMEM] * len(blocks),
        out_shape=jax.ShapeDtypeStruct((count, rows, PAIRS), blocks[0].dtype),
        compiler_params=params(4),
        name="copies",
    )(*after, *blocks)


def mirror_kernel(x, a0, a1, a2, a3, own_ref, other_ref, left, right, rows):
    quarters = (a0, a1, a2, a3)
    for h, wide in enumerate((left, right)):
        lanes = slice(h * 128, h * 128 + 128)
        for i in range(NCOLS):
            block = quarters[i // 6][i % 6, :, lanes]
            wide[pl.ds(i, TILE, stride=PAD), :] = block.astype(jnp.float32)
        for i in range(NCOLS, PAD):
            wide[pl.ds(i, TILE, stride=PAD), :] = jnp.zeros((TILE, 128), jnp.float32)
        rows[:, lanes] = wide[...].astype(jnp.bfloat16)
    for out, base in ((other_ref, HALF), (own_ref, 0)):
        for start in range(0, HALF, CHUNK):
            out[start : start + CHUNK, :] = lax.dot_general(
                x[:, base + start : base + start + CHUNK],
                rows[...],
                (((0,), (0,)), ((), ())),
                preferred_element_type=jnp.float32,
            )


def mirror(x, *quarters):
    half = jax.ShapeDtypeStruct((HALF, PAIRS), jnp.float32)
    return pl.pallas_call(
        mirror_kernel,
        out_shape=(half, half),
        scratch_shapes=[
            pltpu.VMEM((TALL, 128), jnp.float32),
            pltpu.VMEM((TALL, 128), jnp.float32),
            pltpu.VMEM((TALL, PAIRS), jnp.bfloat16),
        ],
        compiler_params=params(16),
        cost_estimate=pl.CostEstimate(
            flops=2 * TALL * WIDE * PAIRS, bytes_accessed=8 * 2**20, transcendentals=0
        ),
        name="mirror",
    )(x, *quarters)


def code(groups, out):
    row = lax.broadcasted_iota(jnp.int32, (EXTRA, PAIRS), 0)
    extra = jnp.zeros((EXTRA, PAIRS), jnp.int32)
    for n, block in enumerate(groups):
        top = jnp.max(jnp.abs(block), axis=0, keepdims=True)
        power = jnp.ceil(jnp.log2(jnp.maximum(top, 2.0**-100)))
        scaled = jnp.floor(block * jnp.exp2(15.0 - power) + 0.5)
        whole = jnp.clip(scaled, -32767.0, 32767.0).astype(jnp.int32)
        out[n * TILE : (n + 1) * TILE, :] = whole.astype(jnp.int16)
        extra = jnp.where(row == n, power.astype(jnp.int32), extra)
    out[len(groups) * TILE :, :] = extra.astype(jnp.int16)


def decode(coded, count):
    extra = coded[count * TILE :, :].astype(jnp.int32).astype(jnp.float32)
    step = jnp.exp2(extra - 15.0)
    return [
        coded[n * TILE : (n + 1) * TILE, :].astype(jnp.int32).astype(jnp.float32)
        * step[n : n + 1, :]
        for n in range(count)
    ]


def direct_kernel(x, own_ref, other_ref, o0, o1, o2, o3, left, right):
    for start in range(0, TALL, CHUNK):
        rows = slice(start, start + CHUNK)
        both = jnp.dot(
            x[rows, :HALF], own_ref[...], preferred_element_type=jnp.float32
        ) + jnp.dot(x[rows, HALF:], other_ref[...], preferred_element_type=jnp.float32)
        left[rows, :] = both[:, :128]
        right[rows, :] = both[:, 128:]

    def block(i):
        rows = pl.ds(i, TILE, stride=PAD)
        return jnp.concatenate([left[rows, :], right[rows, :]], axis=1)

    for q, out in ((1, o1), (2, o2), (3, o3)):
        code([block(q * 6 + n) for n in range(6)], out)
    for n in range(6):
        o0[n * TILE : (n + 1) * TILE, :] = block(n)


def direct(x, own, other):
    coded = jax.ShapeDtypeStruct((LINE + EXTRA, PAIRS), jnp.int16)
    return pl.pallas_call(
        direct_kernel,
        out_shape=(jax.ShapeDtypeStruct((LINE, PAIRS), jnp.float32),) + (coded,) * 3,
        scratch_shapes=[
            pltpu.VMEM((TALL, 128), jnp.float32),
            pltpu.VMEM((TALL, 128), jnp.float32),
        ],
        compiler_params=params(16),
        cost_estimate=pl.CostEstimate(
            flops=2 * TALL * WIDE * PAIRS, bytes_accessed=8 * 2**20, transcendentals=0
        ),
        name="direct",
    )(x, own, other)


def code_y_kernel(keep, got, out):
    @pl.loop(0, 8)
    def _(n):
        rows = pl.multiple_of(n * 2 * TILE, 2 * TILE)
        groups = [
            keep[pl.ds(rows + k * TILE, TILE), :] + got[pl.ds(rows + k * TILE, TILE), :]
            for k in range(2)
        ]
        code(groups, out.at[n])


def code_y(keep, got):
    return pl.pallas_call(
        code_y_kernel,
        out_shape=jax.ShapeDtypeStruct((8, 2 * TILE + EXTRA, PAIRS), jnp.int16),
        compiler_params=params(6),
        name="code_y",
    )(keep, got)


def sum_y_kernel(coded, near, send):
    totals = decode(coded.at[0], 2)
    for n in range(1, 8):
        totals = [a + b for a, b in zip(totals, decode(coded.at[n], 2))]
    near[...], send[...] = totals


def sum_y(coded):
    return pl.pallas_call(
        sum_y_kernel,
        out_shape=(jax.ShapeDtypeStruct((TILE, PAIRS), jnp.float32),) * 2,
        compiler_params=params(4),
        name="sum_y",
    )(coded)


def sum_x_kernel(keep, c1, c2, c3, out):
    parts = [decode(c, 6) for c in (c1, c2, c3)]
    for n in range(6):
        near = keep[n * TILE : (n + 1) * TILE, :]
        code([(near + parts[0][n]) + (parts[1][n] + parts[2][n])], out.at[n])


def sum_x(keep, *coded):
    return pl.pallas_call(
        sum_x_kernel,
        out_shape=jax.ShapeDtypeStruct((6, TILE + EXTRA, PAIRS), jnp.int16),
        compiler_params=params(4),
        name="sum_x",
    )(keep, *coded)


def end_kernel(residual, near, far, coded, out):
    line = [decode(coded.at[n], 1)[0] for n in range(6)]
    a = (line[0] + line[1]) + (line[2] + line[3])
    out[...] = (residual[...] + (near[...] + far[...])) + (a + (line[4] + line[5]))


def end(residual, near, far, line):
    return pl.pallas_call(
        end_kernel,
        out_shape=jax.ShapeDtypeStruct((TILE, PAIRS), jnp.float32),
        compiler_params=params(4),
        name="end",
    )(residual, near, far, line)


SWAP = [(0, 1), (1, 0)]


def swap_x(block, k):
    return lax.ppermute(block, "x", [(i, i ^ k) for i in range(4)])


def trade(block, axis):
    return lax.all_to_all(block, axis, split_axis=0, concat_axis=0)


def per_device(amplitudes, residual_in, v_tiles, tile_map):
    far = lax.ppermute(amplitudes, "zh", SWAP)
    line = trade(jnp.broadcast_to(amplitudes[None], (6, TILE, PAIRS)), "zl")
    x, placed = place(tile_map[0, 0].T, v_tiles[0, 0])
    both = copies(8, (placed,), amplitudes, far)
    own = trade(both, "y").reshape(HALF, PAIRS)
    quarters = [line] + [swap_x(line, k) for k in (1, 2, 3)]
    own, *quarters = lax.optimization_barrier((own, *quarters))

    other = lax.ppermute(own, "co", SWAP)
    keep, send = mirror(x, *quarters)
    got = lax.ppermute(send, "co", SWAP)
    parts = direct(x, own, other)
    got, *parts = lax.optimization_barrier((got, *parts))
    coded_y = code_y(keep, got)
    coded_y, *parts = lax.optimization_barrier((coded_y, *parts))
    row_parts = trade(coded_y, "y")

    col_line = sum_x(parts[0], *(swap_x(parts[k], k) for k in (1, 2, 3)))
    col_line = trade(col_line, "zl")

    row_near, row_send = sum_y(row_parts)
    row_far = lax.ppermute(row_send, "zh", SWAP)
    return end(residual_in, row_near, row_far, col_line)


def solution(mesh):
    fine = Mesh(mesh.devices.reshape(SIZES), AXES)
    return jax.shard_map(
        per_device,
        mesh=fine,
        in_specs=(
            P(AXES, None),
            P(AXES, None),
            P(ROW_AXES, COL_AXES, None, None),
            P(ROW_AXES, COL_AXES, None, None),
        ),
        out_specs=P(AXES, None),
        check_vma=False,
    )
```

```python
import functools

import jax
import jax.numpy as jnp
from jax import lax
from jax.experimental import pallas as pl
from jax.experimental.pallas import tpu as pltpu
from jax.sharding import Mesh, PartitionSpec as P

AXES = ("zh", "y", "co", "zl", "x")
SIZES = (2, 8, 2, 6, 4)
ROW_AXES = ("zh", "y", "co")
COL_AXES = ("zl", "x")
TILE = 48
PAIRS = 256
NCOLS = 24
NROWS = 32
PAD = 32
HALF = NROWS * TILE // 2
WIDE = NROWS * TILE
TALL = PAD * TILE
GROUP = 16
GROUPS = TILE // GROUP
LANES = GROUP * TILE
CHUNK = 256
DEPTH = GROUP * PAD
LINE = 6 * TILE
EXTRA = 16
HBM = pl.BlockSpec(memory_space=pltpu.HBM)
VMEM = pl.BlockSpec(memory_space=pltpu.VMEM)


def params(mib):
    return pltpu.CompilerParams(vmem_limit_bytes=mib * 2**20)


def place_kernel(map_ref, v_hbm, x_hbm, v, x, onehot, dense, v_sem, x_sem):
    slots = v_hbm.shape[0]
    places = NROWS * PAD

    def v_copy(g):
        lanes = pl.ds(pl.multiple_of(g * LANES, LANES), LANES)
        return pltpu.make_async_copy(v_hbm.at[:, lanes], v.at[g], v_sem.at[g])

    def x_copy(g):
        rows = pl.ds(pl.multiple_of(g * DEPTH, DEPTH), DEPTH)
        return pltpu.make_async_copy(x.at[rows, :], x_hbm.at[rows, :], x_sem.at[g])

    for g in range(GROUPS):
        v_copy(g).start()
    my_zh, my_y, my_co = (lax.axis_index(a) for a in ROW_AXES)
    my_x = lax.axis_index("x")
    my_row = my_zh * 16 + my_y * 2 + my_co
    first = map_ref[0:1, :]
    second = map_ref[1:2, :]
    i = first - my_row * NCOLS
    j = (second * 2731) >> 16
    i_place = ((i & 3) ^ my_x) * 6 + (i >> 2)
    j_place = ((j & 1) ^ my_co) * 16 + ((j >> 1) & 7) * 2 + ((j >> 4) ^ my_zh)
    place = j_place * PAD + i_place
    weight = jnp.where(first == second, 0.5, 1.0)
    for start in range(0, places, 128):
        rows = lax.broadcasted_iota(jnp.int32, (128, slots), 0) + start
        onehot[start : start + 128, :] = jnp.where(rows == place, weight, 0.0).astype(
            jnp.bfloat16
        )

    @pl.loop(0, GROUPS)
    def _(g):
        v_copy(g).wait()
        for start in range(0, places, 256):
            dense[start : start + 256, :] = jnp.dot(
                onehot[start : start + 256, :], v[g], preferred_element_type=jnp.float32
            ).astype(jnp.bfloat16)
        for s in range(GROUP):
            parts = [
                dense[j * PAD : (j + 1) * PAD, s * TILE : (s + 1) * TILE] for j in range(NROWS)
            ]
            rows = pl.ds(pl.multiple_of(g * DEPTH + s * PAD, PAD), PAD)
            x[rows, :] = jnp.concatenate(parts, axis=1)
        x_copy(g).start()

    for g in range(GROUPS):
        x_copy(g).wait()


def place(tile_map, v_tiles):
    slots = v_tiles.shape[0]
    return pl.pallas_call(
        place_kernel,
        in_specs=[VMEM, HBM],
        out_specs=HBM,
        out_shape=jax.ShapeDtypeStruct((TALL, WIDE), jnp.bfloat16),
        scratch_shapes=[
            pltpu.VMEM((GROUPS, slots, LANES), jnp.bfloat16),
            pltpu.VMEM((TALL, WIDE), jnp.bfloat16),
            pltpu.VMEM((NROWS * PAD, slots), jnp.bfloat16),
            pltpu.VMEM((NROWS * PAD, LANES), jnp.bfloat16),
            pltpu.SemaphoreType.DMA((GROUPS,)),
            pltpu.SemaphoreType.DMA((GROUPS,)),
        ],
        compiler_params=params(60),
        cost_estimate=pl.CostEstimate(
            flops=2 * 1024 * 512 * 2304, bytes_accessed=8 * 2**20, transcendentals=0
        ),
        name="place",
    )(tile_map, v_tiles)


def copies_kernel(skip, *refs):
    *blocks, out = refs[skip:]
    for n in range(out.shape[0]):
        start = 0
        for block in blocks:
            out[n, start : start + block.shape[0], :] = block[...]
            start += block.shape[0]


def copies(count, after, *blocks):
    rows = sum(b.shape[0] for b in blocks)
    return pl.pallas_call(
        functools.partial(copies_kernel, len(after)),
        in_specs=[pl.BlockSpec(memory_space=pl.ANY)] * len(after) + [VMEM] * len(blocks),
        out_shape=jax.ShapeDtypeStruct((count, rows, PAIRS), blocks[0].dtype),
        compiler_params=params(4),
        name="copies",
    )(*after, *blocks)


def meet_kernel(after, x, block, out):
    out[...] = block[...]


def meet(after, x, block):
    return pl.pallas_call(
        meet_kernel,
        in_specs=[pl.BlockSpec(memory_space=pl.ANY), VMEM, VMEM],
        out_shape=jax.ShapeDtypeStruct(block.shape, block.dtype),
        compiler_params=params(16),
        name="meet",
    )(after, x, block)


def mirror_kernel(x, a0, a1, a2, a3, own_ref, other_ref, left, right, rows):
    quarters = (a0, a1, a2, a3)
    for h, wide in enumerate((left, right)):
        lanes = slice(h * 128, h * 128 + 128)
        for i in range(NCOLS):
            block = quarters[i // 6][i % 6, :, lanes]
            wide[pl.ds(i, TILE, stride=PAD), :] = block.astype(jnp.float32)
        for i in range(NCOLS, PAD):
            wide[pl.ds(i, TILE, stride=PAD), :] = jnp.zeros((TILE, 128), jnp.float32)
        rows[:, lanes] = wide[...].astype(jnp.bfloat16)
    for out, base in ((other_ref, HALF), (own_ref, 0)):
        for start in range(0, HALF, CHUNK):
            out[start : start + CHUNK, :] = lax.dot_general(
                x[:, base + start : base + start + CHUNK],
                rows[...],
                (((0,), (0,)), ((), ())),
                preferred_element_type=jnp.float32,
            )


def mirror(x, *quarters):
    half = jax.ShapeDtypeStruct((HALF, PAIRS), jnp.float32)
    return pl.pallas_call(
        mirror_kernel,
        out_shape=(half, half),
        scratch_shapes=[
            pltpu.VMEM((TALL, 128), jnp.float32),
            pltpu.VMEM((TALL, 128), jnp.float32),
            pltpu.VMEM((TALL, PAIRS), jnp.bfloat16),
        ],
        compiler_params=params(16),
        cost_estimate=pl.CostEstimate(
            flops=2 * TALL * WIDE * PAIRS, bytes_accessed=8 * 2**20, transcendentals=0
        ),
        name="mirror",
    )(x, *quarters)


def code(groups, out):
    row = lax.broadcasted_iota(jnp.int32, (EXTRA, PAIRS), 0)
    extra = jnp.zeros((EXTRA, PAIRS), jnp.int32)
    for n, block in enumerate(groups):
        top = jnp.max(jnp.abs(block), axis=0, keepdims=True)
        power = jnp.ceil(jnp.log2(jnp.maximum(top, 2.0**-100)))
        scaled = jnp.floor(block * jnp.exp2(15.0 - power) + 0.5)
        whole = jnp.clip(scaled, -32767.0, 32767.0).astype(jnp.int32)
        out[n * TILE : (n + 1) * TILE, :] = whole.astype(jnp.int16)
        extra = jnp.where(row == n, power.astype(jnp.int32), extra)
    out[len(groups) * TILE :, :] = extra.astype(jnp.int16)


def decode(coded, count):
    extra = coded[count * TILE :, :].astype(jnp.int32).astype(jnp.float32)
    step = jnp.exp2(extra - 15.0)
    return [
        coded[n * TILE : (n + 1) * TILE, :].astype(jnp.int32).astype(jnp.float32)
        * step[n : n + 1, :]
        for n in range(count)
    ]


def direct_kernel(x, own_ref, other_ref, o0, o1, o2, o3, left, right):
    for start in range(0, TALL, CHUNK):
        rows = slice(start, start + CHUNK)
        both = jnp.dot(
            x[rows, :HALF], own_ref[...], preferred_element_type=jnp.float32
        ) + jnp.dot(x[rows, HALF:], other_ref[...], preferred_element_type=jnp.float32)
        left[rows, :] = both[:, :128]
        right[rows, :] = both[:, 128:]

    def block(i):
        rows = pl.ds(i, TILE, stride=PAD)
        return jnp.concatenate([left[rows, :], right[rows, :]], axis=1)

    for q, out in ((1, o1), (2, o2), (3, o3)):
        code([block(q * 6 + n) for n in range(6)], out)
    for n in range(6):
        o0[n * TILE : (n + 1) * TILE, :] = block(n)


def direct(x, own, other):
    coded = jax.ShapeDtypeStruct((LINE + EXTRA, PAIRS), jnp.int16)
    return pl.pallas_call(
        direct_kernel,
        out_shape=(jax.ShapeDtypeStruct((LINE, PAIRS), jnp.float32),) + (coded,) * 3,
        scratch_shapes=[
            pltpu.VMEM((TALL, 128), jnp.float32),
            pltpu.VMEM((TALL, 128), jnp.float32),
        ],
        compiler_params=params(16),
        cost_estimate=pl.CostEstimate(
            flops=2 * TALL * WIDE * PAIRS, bytes_accessed=8 * 2**20, transcendentals=0
        ),
        name="direct",
    )(x, own, other)


def code_y_kernel(keep, got, out):
    @pl.loop(0, 8)
    def _(n):
        rows = pl.multiple_of(n * 2 * TILE, 2 * TILE)
        groups = [
            keep[pl.ds(rows + k * TILE, TILE), :] + got[pl.ds(rows + k * TILE, TILE), :]
            for k in range(2)
        ]
        code(groups, out.at[n])


def code_y(keep, got):
    return pl.pallas_call(
        code_y_kernel,
        out_shape=jax.ShapeDtypeStruct((8, 2 * TILE + EXTRA, PAIRS), jnp.int16),
        compiler_params=params(6),
        name="code_y",
    )(keep, got)


def sum_y_kernel(coded, near, send):
    totals = decode(coded.at[0], 2)
    for n in range(1, 8):
        totals = [a + b for a, b in zip(totals, decode(coded.at[n], 2))]
    near[...], send[...] = totals


def sum_y(coded):
    return pl.pallas_call(
        sum_y_kernel,
        out_shape=(jax.ShapeDtypeStruct((TILE, PAIRS), jnp.float32),) * 2,
        compiler_params=params(4),
        name="sum_y",
    )(coded)


def sum_x_kernel(keep, c1, c2, c3, out):
    parts = [decode(c, 6) for c in (c1, c2, c3)]
    for n in range(6):
        near = keep[n * TILE : (n + 1) * TILE, :]
        code([(near + parts[0][n]) + (parts[1][n] + parts[2][n])], out.at[n])


def sum_x(keep, *coded):
    return pl.pallas_call(
        sum_x_kernel,
        out_shape=jax.ShapeDtypeStruct((6, TILE + EXTRA, PAIRS), jnp.int16),
        compiler_params=params(4),
        name="sum_x",
    )(keep, *coded)


def end_kernel(residual, near, far, coded, out):
    line = [decode(coded.at[n], 1)[0] for n in range(6)]
    a = (line[0] + line[1]) + (line[2] + line[3])
    out[...] = (residual[...] + (near[...] + far[...])) + (a + (line[4] + line[5]))


def end(residual, near, far, line):
    return pl.pallas_call(
        end_kernel,
        out_shape=jax.ShapeDtypeStruct((TILE, PAIRS), jnp.float32),
        compiler_params=params(4),
        name="end",
    )(residual, near, far, line)


SWAP = [(0, 1), (1, 0)]


def swap_x(block, k):
    return lax.ppermute(block, "x", [(i, i ^ k) for i in range(4)])


def trade(block, axis):
    return lax.all_to_all(block, axis, split_axis=0, concat_axis=0)


def per_device(amplitudes, residual_in, v_tiles, tile_map):
    far = lax.ppermute(amplitudes, "zh", SWAP)
    line = trade(copies(6, (), amplitudes), "zl")
    x = place(tile_map[0, 0].T, v_tiles[0, 0])
    x, far = lax.optimization_barrier((x, far))
    own = trade(copies(8, (), amplitudes, far), "y").reshape(HALF, PAIRS)
    quarters = [swap_x(line, k) for k in (1, 2, 3)]
    near = meet(own, x, line)
    quarters = [near] + quarters

    other = lax.ppermute(own, "co", SWAP)
    keep, send = mirror(x, *quarters)
    got = lax.ppermute(send, "co", SWAP)
    parts = direct(x, own, other)
    got, *parts = lax.optimization_barrier((got, *parts))
    coded_y = code_y(keep, got)
    coded_y, *parts = lax.optimization_barrier((coded_y, *parts))
    row_parts = trade(coded_y, "y")

    col_line = sum_x(parts[0], *(swap_x(parts[k], k) for k in (1, 2, 3)))
    col_line = trade(col_line, "zl")

    row_near, row_send = sum_y(row_parts)
    row_far = lax.ppermute(row_send, "zh", SWAP)
    return end(residual_in, row_near, row_far, col_line)


def solution(mesh):
    fine = Mesh(mesh.devices.reshape(SIZES), AXES)
    return jax.shard_map(
        per_device,
        mesh=fine,
        in_specs=(
            P(AXES, None),
            P(AXES, None),
            P(ROW_AXES, COL_AXES, None, None),
            P(ROW_AXES, COL_AXES, None, None),
        ),
        out_specs=P(AXES, None),
        check_vma=False,
    )
```

```python
import functools

import jax
import jax.numpy as jnp
from jax import lax
from jax.experimental import pallas as pl
from jax.experimental.pallas import tpu as pltpu
from jax.sharding import Mesh, PartitionSpec as P

AXES = ("zh", "y", "co", "zl", "x")
SIZES = (2, 8, 2, 6, 4)
ROW_AXES = ("zh", "y", "co")
COL_AXES = ("zl", "x")
TILE = 48
PAIRS = 256
NCOLS = 24
NROWS = 32
PAD = 32
HALF = NROWS * TILE // 2
WIDE = NROWS * TILE
TALL = PAD * TILE
GROUP = 16
GROUPS = TILE // GROUP
LANES = GROUP * TILE
CHUNK = 256
DEPTH = GROUP * PAD
LINE = 6 * TILE
EXTRA = 16
HBM = pl.BlockSpec(memory_space=pltpu.HBM)
VMEM = pl.BlockSpec(memory_space=pltpu.VMEM)


def params(mib):
    return pltpu.CompilerParams(vmem_limit_bytes=mib * 2**20)


def place_kernel(map_ref, v_hbm, x_hbm, v, x, onehot, dense, v_sem, x_sem):
    slots = v_hbm.shape[0]
    places = NROWS * PAD

    def v_copy(g):
        lanes = pl.ds(pl.multiple_of(g * LANES, LANES), LANES)
        return pltpu.make_async_copy(v_hbm.at[:, lanes], v.at[g], v_sem.at[g])

    def x_copy(g):
        rows = pl.ds(pl.multiple_of(g * DEPTH, DEPTH), DEPTH)
        return pltpu.make_async_copy(x.at[rows, :], x_hbm.at[rows, :], x_sem.at[g])

    for g in range(GROUPS):
        v_copy(g).start()
    my_zh, my_y, my_co = (lax.axis_index(a) for a in ROW_AXES)
    my_x = lax.axis_index("x")
    my_row = my_zh * 16 + my_y * 2 + my_co
    first = map_ref[0:1, :]
    second = map_ref[1:2, :]
    i = first - my_row * NCOLS
    j = (second * 2731) >> 16
    i_place = ((i & 3) ^ my_x) * 6 + (i >> 2)
    j_place = ((j & 1) ^ my_co) * 16 + ((j >> 1) & 7) * 2 + ((j >> 4) ^ my_zh)
    place = j_place * PAD + i_place
    weight = jnp.where(first == second, 0.5, 1.0)
    for start in range(0, places, 128):
        rows = lax.broadcasted_iota(jnp.int32, (128, slots), 0) + start
        onehot[start : start + 128, :] = jnp.where(rows == place, weight, 0.0).astype(
            jnp.bfloat16
        )

    @pl.loop(0, GROUPS)
    def _(g):
        v_copy(g).wait()
        for start in range(0, places, 256):
            dense[start : start + 256, :] = jnp.dot(
                onehot[start : start + 256, :], v[g], preferred_element_type=jnp.float32
            ).astype(jnp.bfloat16)
        for s in range(GROUP):
            parts = [
                dense[j * PAD : (j + 1) * PAD, s * TILE : (s + 1) * TILE] for j in range(NROWS)
            ]
            rows = pl.ds(pl.multiple_of(g * DEPTH + s * PAD, PAD), PAD)
            x[rows, :] = jnp.concatenate(parts, axis=1)
        x_copy(g).start()

    for g in range(GROUPS):
        x_copy(g).wait()


def place(tile_map, v_tiles):
    slots = v_tiles.shape[0]
    return pl.pallas_call(
        place_kernel,
        in_specs=[VMEM, HBM],
        out_specs=HBM,
        out_shape=jax.ShapeDtypeStruct((TALL, WIDE), jnp.bfloat16),
        scratch_shapes=[
            pltpu.VMEM((GROUPS, slots, LANES), jnp.bfloat16),
            pltpu.VMEM((TALL, WIDE), jnp.bfloat16),
            pltpu.VMEM((NROWS * PAD, slots), jnp.bfloat16),
            pltpu.VMEM((NROWS * PAD, LANES), jnp.bfloat16),
            pltpu.SemaphoreType.DMA((GROUPS,)),
            pltpu.SemaphoreType.DMA((GROUPS,)),
        ],
        compiler_params=params(60),
        cost_estimate=pl.CostEstimate(
            flops=2 * 1024 * 512 * 2304, bytes_accessed=8 * 2**20, transcendentals=0
        ),
        name="place",
    )(tile_map, v_tiles)


def copies_kernel(skip, *refs):
    *blocks, out = refs[skip:]
    for n in range(out.shape[0]):
        start = 0
        for block in blocks:
            out[n, start : start + block.shape[0], :] = block[...]
            start += block.shape[0]


def copies(count, after, *blocks):
    rows = sum(b.shape[0] for b in blocks)
    return pl.pallas_call(
        functools.partial(copies_kernel, len(after)),
        in_specs=[pl.BlockSpec(memory_space=pl.ANY)] * len(after) + [VMEM] * len(blocks),
        out_shape=jax.ShapeDtypeStruct((count, rows, PAIRS), blocks[0].dtype),
        compiler_params=params(4),
        name="copies",
    )(*after, *blocks)


def meet_kernel(after, x, block, out):
    out[...] = block[...]


def meet(after, x, block):
    return pl.pallas_call(
        meet_kernel,
        in_specs=[pl.BlockSpec(memory_space=pl.ANY), VMEM, VMEM],
        out_shape=jax.ShapeDtypeStruct(block.shape, block.dtype),
        compiler_params=params(16),
        name="meet",
    )(after, x, block)


def mirror_kernel(x, a0, a1, a2, a3, own_ref, other_ref, left, right, rows):
    quarters = (a0, a1, a2, a3)
    for h, wide in enumerate((left, right)):
        lanes = slice(h * 128, h * 128 + 128)
        for i in range(NCOLS):
            block = quarters[i // 6][i % 6, :, lanes]
            wide[pl.ds(i, TILE, stride=PAD), :] = block.astype(jnp.float32)
        for i in range(NCOLS, PAD):
            wide[pl.ds(i, TILE, stride=PAD), :] = jnp.zeros((TILE, 128), jnp.float32)
        rows[:, lanes] = wide[...].astype(jnp.bfloat16)
    for out, base in ((other_ref, HALF), (own_ref, 0)):
        for start in range(0, HALF, CHUNK):
            out[start : start + CHUNK, :] = lax.dot_general(
                x[:, base + start : base + start + CHUNK],
                rows[...],
                (((0,), (0,)), ((), ())),
                preferred_element_type=jnp.float32,
            )


def mirror(x, *quarters):
    half = jax.ShapeDtypeStruct((HALF, PAIRS), jnp.float32)
    return pl.pallas_call(
        mirror_kernel,
        out_shape=(half, half),
        scratch_shapes=[
            pltpu.VMEM((TALL, 128), jnp.float32),
            pltpu.VMEM((TALL, 128), jnp.float32),
            pltpu.VMEM((TALL, PAIRS), jnp.bfloat16),
        ],
        compiler_params=params(16),
        cost_estimate=pl.CostEstimate(
            flops=2 * TALL * WIDE * PAIRS, bytes_accessed=8 * 2**20, transcendentals=0
        ),
        name="mirror",
    )(x, *quarters)


def code(groups, out):
    row = lax.broadcasted_iota(jnp.int32, (EXTRA, PAIRS), 0)
    extra = jnp.zeros((EXTRA, PAIRS), jnp.int32)
    for n, block in enumerate(groups):
        top = jnp.max(jnp.abs(block), axis=0, keepdims=True)
        power = jnp.ceil(jnp.log2(jnp.maximum(top, 2.0**-100)))
        scaled = jnp.floor(block * jnp.exp2(15.0 - power) + 0.5)
        whole = jnp.clip(scaled, -32767.0, 32767.0).astype(jnp.int32)
        out[n * TILE : (n + 1) * TILE, :] = whole.astype(jnp.int16)
        extra = jnp.where(row == n, power.astype(jnp.int32), extra)
    out[len(groups) * TILE :, :] = extra.astype(jnp.int16)


def decode(coded, count):
    extra = coded[count * TILE :, :].astype(jnp.int32).astype(jnp.float32)
    step = jnp.exp2(extra - 15.0)
    return [
        coded[n * TILE : (n + 1) * TILE, :].astype(jnp.int32).astype(jnp.float32)
        * step[n : n + 1, :]
        for n in range(count)
    ]


def direct_kernel(x, own_ref, other_ref, o0, o3, coded, left, right):
    for start in range(0, TALL, CHUNK):
        rows = slice(start, start + CHUNK)
        both = jnp.dot(
            x[rows, :HALF], own_ref[...], preferred_element_type=jnp.float32
        ) + jnp.dot(x[rows, HALF:], other_ref[...], preferred_element_type=jnp.float32)
        left[rows, :] = both[:, :128]
        right[rows, :] = both[:, 128:]

    def block(i):
        rows = pl.ds(i, TILE, stride=PAD)
        return jnp.concatenate([left[rows, :], right[rows, :]], axis=1)

    for q in (1, 2):
        code([block(q * 6 + n) for n in range(6)], coded.at[q - 1])
    for q, out in ((0, o0), (3, o3)):
        for n in range(6):
            out[n * TILE : (n + 1) * TILE, :] = block(q * 6 + n)


def direct(x, own, other):
    line = jax.ShapeDtypeStruct((LINE, PAIRS), jnp.float32)
    coded = jax.ShapeDtypeStruct((2, LINE + EXTRA, PAIRS), jnp.int16)
    return pl.pallas_call(
        direct_kernel,
        out_shape=(line, line, coded),
        scratch_shapes=[
            pltpu.VMEM((TALL, 128), jnp.float32),
            pltpu.VMEM((TALL, 128), jnp.float32),
        ],
        compiler_params=params(16),
        cost_estimate=pl.CostEstimate(
            flops=2 * TALL * WIDE * PAIRS, bytes_accessed=8 * 2**20, transcendentals=0
        ),
        name="direct",
    )(x, own, other)


def code_y_kernel(keep, got, out):
    @pl.loop(0, 8)
    def _(n):
        rows = pl.multiple_of(n * 2 * TILE, 2 * TILE)
        groups = [
            keep[pl.ds(rows + k * TILE, TILE), :] + got[pl.ds(rows + k * TILE, TILE), :]
            for k in range(2)
        ]
        code(groups, out.at[n])


def code_y(keep, got):
    return pl.pallas_call(
        code_y_kernel,
        out_shape=jax.ShapeDtypeStruct((8, 2 * TILE + EXTRA, PAIRS), jnp.int16),
        compiler_params=params(6),
        name="code_y",
    )(keep, got)


def sum_y_kernel(coded, near, send):
    totals = decode(coded.at[0], 2)
    for n in range(1, 8):
        totals = [a + b for a, b in zip(totals, decode(coded.at[n], 2))]
    near[...], send[...] = totals


def sum_y(coded):
    return pl.pallas_call(
        sum_y_kernel,
        out_shape=(jax.ShapeDtypeStruct((TILE, PAIRS), jnp.float32),) * 2,
        compiler_params=params(4),
        name="sum_y",
    )(coded)


def half_x_kernel(o0, o3, got, near, send):
    first, second = decode(got.at[0], 6), decode(got.at[1], 6)
    for n in range(6):
        rows = slice(n * TILE, (n + 1) * TILE)
        near[rows, :] = o0[rows, :] + first[n]
    code([o3[n * TILE : (n + 1) * TILE, :] + second[n] for n in range(6)], send)


def half_x(o0, o3, got):
    return pl.pallas_call(
        half_x_kernel,
        out_shape=(
            jax.ShapeDtypeStruct((LINE, PAIRS), jnp.float32),
            jax.ShapeDtypeStruct((LINE + EXTRA, PAIRS), jnp.int16),
        ),
        compiler_params=params(6),
        name="half_x",
    )(o0, o3, got)


def sum_x_kernel(near, got, out):
    parts = decode(got, 6)
    for n in range(6):
        code([near[n * TILE : (n + 1) * TILE, :] + parts[n]], out.at[n])


def sum_x(near, got):
    return pl.pallas_call(
        sum_x_kernel,
        out_shape=jax.ShapeDtypeStruct((6, TILE + EXTRA, PAIRS), jnp.int16),
        compiler_params=params(4),
        name="sum_x",
    )(near, got)


def end_kernel(residual, near, far, coded, out):
    line = [decode(coded.at[n], 1)[0] for n in range(6)]
    a = (line[0] + line[1]) + (line[2] + line[3])
    out[...] = (residual[...] + (near[...] + far[...])) + (a + (line[4] + line[5]))


def end(residual, near, far, line):
    return pl.pallas_call(
        end_kernel,
        out_shape=jax.ShapeDtypeStruct((TILE, PAIRS), jnp.float32),
        compiler_params=params(4),
        name="end",
    )(residual, near, far, line)


SWAP = [(0, 1), (1, 0)]


def swap_x(block, k):
    return lax.ppermute(block, "x", [(i, i ^ k) for i in range(4)])


def trade(block, axis):
    return lax.all_to_all(block, axis, split_axis=0, concat_axis=0)


def per_device(amplitudes, residual_in, v_tiles, tile_map):
    far = lax.ppermute(amplitudes, "zh", SWAP)
    line = trade(copies(6, (), amplitudes), "zl")
    x = place(tile_map[0, 0].T, v_tiles[0, 0])
    x, far = lax.optimization_barrier((x, far))
    own = trade(copies(8, (), amplitudes, far), "y").reshape(HALF, PAIRS)
    quarters = [meet(own, x, line)] + [swap_x(line, k) for k in (1, 2, 3)]
    own, *quarters = lax.optimization_barrier((own, *quarters))

    other = lax.ppermute(own, "co", SWAP)
    o0, o3, pair = direct(x, own, other)
    o0, *quarters = lax.optimization_barrier((o0, *quarters))
    beside = swap_x(pair, 1)

    keep, send = mirror(x, *quarters)
    send, beside = lax.optimization_barrier((send, beside))
    got = lax.ppermute(send, "co", SWAP)
    near, last = half_x(o0, o3, beside)
    got, near, last = lax.optimization_barrier((got, near, last))
    row_parts = trade(code_y(keep, got), "y")
    col_line = sum_x(near, swap_x(last, 3))
    col_line = trade(col_line, "zl")

    row_near, row_send = sum_y(row_parts)
    row_far = lax.ppermute(row_send, "zh", SWAP)
    return end(residual_in, row_near, row_far, col_line)


def solution(mesh):
    fine = Mesh(mesh.devices.reshape(SIZES), AXES)
    return jax.shard_map(
        per_device,
        mesh=fine,
        in_specs=(
            P(AXES, None),
            P(AXES, None),
            P(ROW_AXES, COL_AXES, None, None),
            P(ROW_AXES, COL_AXES, None, None),
        ),
        out_specs=P(AXES, None),
        check_vma=False,
    )
```

```python
import functools

import jax
import jax.numpy as jnp
from jax import lax
from jax.experimental import pallas as pl
from jax.experimental.pallas import tpu as pltpu
from jax.sharding import Mesh, PartitionSpec as P

AXES = ("zh", "y", "co", "zl", "x")
SIZES = (2, 8, 2, 6, 4)
ROW_AXES = ("zh", "y", "co")
COL_AXES = ("zl", "x")
TILE = 48
PAIRS = 256
NCOLS = 24
NROWS = 32
PAD = 32
HALF = NROWS * TILE // 2
WIDE = NROWS * TILE
TALL = PAD * TILE
GROUP = 16
GROUPS = TILE // GROUP
LANES = GROUP * TILE
CHUNK = 256
DEPTH = GROUP * PAD
LINE = 6 * TILE
EXTRA = 16
HBM = pl.BlockSpec(memory_space=pltpu.HBM)
VMEM = pl.BlockSpec(memory_space=pltpu.VMEM)


def params(mib):
    return pltpu.CompilerParams(vmem_limit_bytes=mib * 2**20)


def place_kernel(map_ref, v_hbm, x_hbm, v, x, onehot, dense, v_sem, x_sem):
    slots = v_hbm.shape[0]
    places = NROWS * PAD

    def v_copy(g):
        lanes = pl.ds(pl.multiple_of(g * LANES, LANES), LANES)
        return pltpu.make_async_copy(v_hbm.at[:, lanes], v.at[g], v_sem.at[g])

    def x_copy(g):
        rows = pl.ds(pl.multiple_of(g * DEPTH, DEPTH), DEPTH)
        return pltpu.make_async_copy(x.at[rows, :], x_hbm.at[rows, :], x_sem.at[g])

    for g in range(GROUPS):
        v_copy(g).start()
    my_zh, my_y, my_co = (lax.axis_index(a) for a in ROW_AXES)
    my_x = lax.axis_index("x")
    my_row = my_zh * 16 + my_y * 2 + my_co
    first = map_ref[0:1, :]
    second = map_ref[1:2, :]
    i = first - my_row * NCOLS
    j = (second * 2731) >> 16
    i_place = ((i & 3) ^ my_x) * 6 + (i >> 2)
    j_place = ((j & 1) ^ my_co) * 16 + ((j >> 1) & 7) * 2 + ((j >> 4) ^ my_zh)
    place = j_place * PAD + i_place
    weight = jnp.where(first == second, 0.5, 1.0)
    for start in range(0, places, 128):
        rows = lax.broadcasted_iota(jnp.int32, (128, slots), 0) + start
        onehot[start : start + 128, :] = jnp.where(rows == place, weight, 0.0).astype(
            jnp.bfloat16
        )

    @pl.loop(0, GROUPS)
    def _(g):
        v_copy(g).wait()
        for start in range(0, places, 256):
            dense[start : start + 256, :] = jnp.dot(
                onehot[start : start + 256, :], v[g], preferred_element_type=jnp.float32
            ).astype(jnp.bfloat16)
        for s in range(GROUP):
            parts = [
                dense[j * PAD : (j + 1) * PAD, s * TILE : (s + 1) * TILE] for j in range(NROWS)
            ]
            rows = pl.ds(pl.multiple_of(g * DEPTH + s * PAD, PAD), PAD)
            x[rows, :] = jnp.concatenate(parts, axis=1)
        x_copy(g).start()

    for g in range(GROUPS):
        x_copy(g).wait()


def place(tile_map, v_tiles):
    slots = v_tiles.shape[0]
    return pl.pallas_call(
        place_kernel,
        in_specs=[VMEM, HBM],
        out_specs=HBM,
        out_shape=jax.ShapeDtypeStruct((TALL, WIDE), jnp.bfloat16),
        scratch_shapes=[
            pltpu.VMEM((GROUPS, slots, LANES), jnp.bfloat16),
            pltpu.VMEM((TALL, WIDE), jnp.bfloat16),
            pltpu.VMEM((NROWS * PAD, slots), jnp.bfloat16),
            pltpu.VMEM((NROWS * PAD, LANES), jnp.bfloat16),
            pltpu.SemaphoreType.DMA((GROUPS,)),
            pltpu.SemaphoreType.DMA((GROUPS,)),
        ],
        compiler_params=params(60),
        cost_estimate=pl.CostEstimate(
            flops=2 * 1024 * 512 * 2304, bytes_accessed=8 * 2**20, transcendentals=0
        ),
        name="place",
    )(tile_map, v_tiles)


def copies_kernel(skip, *refs):
    *blocks, out = refs[skip:]
    for n in range(out.shape[0]):
        start = 0
        for block in blocks:
            out[n, start : start + block.shape[0], :] = block[...]
            start += block.shape[0]


def copies(count, after, *blocks):
    rows = sum(b.shape[0] for b in blocks)
    return pl.pallas_call(
        functools.partial(copies_kernel, len(after)),
        in_specs=[pl.BlockSpec(memory_space=pl.ANY)] * len(after) + [VMEM] * len(blocks),
        out_shape=jax.ShapeDtypeStruct((count, rows, PAIRS), blocks[0].dtype),
        compiler_params=params(4),
        name="copies",
    )(*after, *blocks)


def six_kernel(block, out, sem):
    moves = [pltpu.make_async_copy(block, out.at[n], sem.at[n]) for n in range(6)]
    for move in moves:
        move.start()
    for move in moves:
        move.wait()


def six(block):
    return pl.pallas_call(
        six_kernel,
        in_specs=[HBM],
        out_specs=HBM,
        out_shape=jax.ShapeDtypeStruct((6,) + block.shape, block.dtype),
        scratch_shapes=[pltpu.SemaphoreType.DMA((6,))],
        compiler_params=params(60),
        name="six",
    )(block)


def mirror_kernel(x, a0, a1, a2, a3, own_ref, other_ref, left, right, rows):
    quarters = (a0, a1, a2, a3)
    for h, wide in enumerate((left, right)):
        lanes = slice(h * 128, h * 128 + 128)
        for i in range(NCOLS):
            block = quarters[i // 6][i % 6, :, lanes]
            wide[pl.ds(i, TILE, stride=PAD), :] = block.astype(jnp.float32)
        for i in range(NCOLS, PAD):
            wide[pl.ds(i, TILE, stride=PAD), :] = jnp.zeros((TILE, 128), jnp.float32)
        rows[:, lanes] = wide[...].astype(jnp.bfloat16)
    for out, base in ((other_ref, HALF), (own_ref, 0)):
        for start in range(0, HALF, CHUNK):
            out[start : start + CHUNK, :] = lax.dot_general(
                x[:, base + start : base + start + CHUNK],
                rows[...],
                (((0,), (0,)), ((), ())),
                preferred_element_type=jnp.float32,
            )


def mirror(x, *quarters):
    half = jax.ShapeDtypeStruct((HALF, PAIRS), jnp.float32)
    return pl.pallas_call(
        mirror_kernel,
        out_shape=(half, half),
        scratch_shapes=[
            pltpu.VMEM((TALL, 128), jnp.float32),
            pltpu.VMEM((TALL, 128), jnp.float32),
            pltpu.VMEM((TALL, PAIRS), jnp.bfloat16),
        ],
        compiler_params=params(16),
        cost_estimate=pl.CostEstimate(
            flops=2 * TALL * WIDE * PAIRS, bytes_accessed=8 * 2**20, transcendentals=0
        ),
        name="mirror",
    )(x, *quarters)


def code(groups, out):
    row = lax.broadcasted_iota(jnp.int32, (EXTRA, PAIRS), 0)
    extra = jnp.zeros((EXTRA, PAIRS), jnp.int32)
    for n, block in enumerate(groups):
        top = jnp.max(jnp.abs(block), axis=0, keepdims=True)
        power = jnp.ceil(jnp.log2(jnp.maximum(top, 2.0**-100)))
        scaled = jnp.floor(block * jnp.exp2(15.0 - power) + 0.5)
        whole = jnp.clip(scaled, -32767.0, 32767.0).astype(jnp.int32)
        out[n * TILE : (n + 1) * TILE, :] = whole.astype(jnp.int16)
        extra = jnp.where(row == n, power.astype(jnp.int32), extra)
    out[len(groups) * TILE :, :] = extra.astype(jnp.int16)


def decode(coded, count):
    extra = coded[count * TILE :, :].astype(jnp.int32).astype(jnp.float32)
    step = jnp.exp2(extra - 15.0)
    return [
        coded[n * TILE : (n + 1) * TILE, :].astype(jnp.int32).astype(jnp.float32)
        * step[n : n + 1, :]
        for n in range(count)
    ]


def direct_kernel(x, own_ref, other_ref, o0, o1, o2, o3, left, right):
    for start in range(0, TALL, CHUNK):
        rows = slice(start, start + CHUNK)
        both = jnp.dot(
            x[rows, :HALF], own_ref[...], preferred_element_type=jnp.float32
        ) + jnp.dot(x[rows, HALF:], other_ref[...], preferred_element_type=jnp.float32)
        left[rows, :] = both[:, :128]
        right[rows, :] = both[:, 128:]

    def block(i):
        rows = pl.ds(i, TILE, stride=PAD)
        return jnp.concatenate([left[rows, :], right[rows, :]], axis=1)

    for q, out in ((1, o1), (2, o2), (3, o3)):
        code([block(q * 6 + n) for n in range(6)], out)
    for n in range(6):
        o0[n * TILE : (n + 1) * TILE, :] = block(n)


def direct(x, own, other):
    coded = jax.ShapeDtypeStruct((LINE + EXTRA, PAIRS), jnp.int16)
    return pl.pallas_call(
        direct_kernel,
        out_shape=(jax.ShapeDtypeStruct((LINE, PAIRS), jnp.float32),) + (coded,) * 3,
        scratch_shapes=[
            pltpu.VMEM((TALL, 128), jnp.float32),
            pltpu.VMEM((TALL, 128), jnp.float32),
        ],
        compiler_params=params(16),
        cost_estimate=pl.CostEstimate(
            flops=2 * TALL * WIDE * PAIRS, bytes_accessed=8 * 2**20, transcendentals=0
        ),
        name="direct",
    )(x, own, other)


def code_y_kernel(keep, got, out):
    @pl.loop(0, 8)
    def _(n):
        rows = pl.multiple_of(n * 2 * TILE, 2 * TILE)
        groups = [
            keep[pl.ds(rows + k * TILE, TILE), :] + got[pl.ds(rows + k * TILE, TILE), :]
            for k in range(2)
        ]
        code(groups, out.at[n])


def code_y(keep, got):
    return pl.pallas_call(
        code_y_kernel,
        out_shape=jax.ShapeDtypeStruct((8, 2 * TILE + EXTRA, PAIRS), jnp.int16),
        compiler_params=params(6),
        name="code_y",
    )(keep, got)


def sum_y_kernel(coded, near, send):
    totals = decode(coded.at[0], 2)
    for n in range(1, 8):
        totals = [a + b for a, b in zip(totals, decode(coded.at[n], 2))]
    near[...] = totals[0]
    code([totals[1]], send)


def sum_y(coded):
    return pl.pallas_call(
        sum_y_kernel,
        out_shape=(
            jax.ShapeDtypeStruct((TILE, PAIRS), jnp.float32),
            jax.ShapeDtypeStruct((TILE + EXTRA, PAIRS), jnp.int16),
        ),
        compiler_params=params(4),
        name="sum_y",
    )(coded)


def sum_x_kernel(keep, c1, c2, c3, out):
    parts = [decode(c, 6) for c in (c1, c2, c3)]
    for n in range(6):
        near = keep[n * TILE : (n + 1) * TILE, :]
        code([(near + parts[0][n]) + (parts[1][n] + parts[2][n])], out.at[n])


def sum_x(keep, *coded):
    return pl.pallas_call(
        sum_x_kernel,
        out_shape=jax.ShapeDtypeStruct((6, TILE + EXTRA, PAIRS), jnp.int16),
        compiler_params=params(4),
        name="sum_x",
    )(keep, *coded)


def end_kernel(residual, near, far, coded, out):
    line = [decode(coded.at[n], 1)[0] for n in range(6)]
    a = (line[0] + line[1]) + (line[2] + line[3])
    out[...] = (residual[...] + (near[...] + decode(far, 1)[0])) + (a + (line[4] + line[5]))


def end(residual, near, far, line):
    return pl.pallas_call(
        end_kernel,
        out_shape=jax.ShapeDtypeStruct((TILE, PAIRS), jnp.float32),
        compiler_params=params(4),
        name="end",
    )(residual, near, far, line)


SWAP = [(0, 1), (1, 0)]


def swap_x(block, k):
    return lax.ppermute(block, "x", [(i, i ^ k) for i in range(4)])


def trade(block, axis):
    return lax.all_to_all(block, axis, split_axis=0, concat_axis=0)


def per_device(amplitudes, residual_in, v_tiles, tile_map):
    far = lax.ppermute(amplitudes, "zh", SWAP)
    line = trade(six(amplitudes), "zl")
    x = place(tile_map[0, 0].T, v_tiles[0, 0])
    x, far = lax.optimization_barrier((x, far))
    own = trade(copies(8, (), amplitudes, far), "y").reshape(HALF, PAIRS)
    quarters = [swap_x(line, k) for k in (1, 2, 3)]
    keep, send = mirror(x, line, *quarters)
    send, own = lax.optimization_barrier((send, own))
    other = lax.ppermute(own, "co", SWAP)
    got = lax.ppermute(send, "co", SWAP)
    coded_y = code_y(keep, got)
    coded_y, other = lax.optimization_barrier((coded_y, other))
    row_parts = trade(coded_y, "y")

    parts = direct(x, own, other)
    col_line = sum_x(parts[0], *(swap_x(parts[k], k) for k in (1, 2, 3)))
    col_line = trade(col_line, "zl")

    row_near, row_send = sum_y(row_parts)
    row_far = lax.ppermute(row_send, "zh", SWAP)
    return end(residual_in, row_near, row_far, col_line)


def solution(mesh):
    fine = Mesh(mesh.devices.reshape(SIZES), AXES)
    return jax.shard_map(
        per_device,
        mesh=fine,
        in_specs=(
            P(AXES, None),
            P(AXES, None),
            P(ROW_AXES, COL_AXES, None, None),
            P(ROW_AXES, COL_AXES, None, None),
        ),
        out_specs=P(AXES, None),
        check_vma=False,
    )
```

```python
import functools

import jax
import jax.numpy as jnp
from jax import lax
from jax.experimental import pallas as pl
from jax.experimental.pallas import tpu as pltpu
from jax.sharding import Mesh, PartitionSpec as P

AXES = ("zh", "y", "co", "zl", "x")
SIZES = (2, 8, 2, 6, 4)
ROW_AXES = ("zh", "y", "co")
COL_AXES = ("zl", "x")
TILE = 48
PAIRS = 256
NCOLS = 24
NROWS = 32
PAD = 32
HALF = NROWS * TILE // 2
WIDE = NROWS * TILE
TALL = PAD * TILE
GROUP = 16
GROUPS = TILE // GROUP
LANES = GROUP * TILE
CHUNK = 256
DEPTH = GROUP * PAD
LINE = 6 * TILE
EXTRA = 16
HBM = pl.BlockSpec(memory_space=pltpu.HBM)
VMEM = pl.BlockSpec(memory_space=pltpu.VMEM)


def params(mib):
    return pltpu.CompilerParams(vmem_limit_bytes=mib * 2**20)


def place_kernel(map_ref, v_hbm, x_hbm, v, x, onehot, dense, v_sem, x_sem):
    slots = v_hbm.shape[0]
    places = NROWS * PAD

    def v_copy(g):
        lanes = pl.ds(pl.multiple_of(g * LANES, LANES), LANES)
        return pltpu.make_async_copy(v_hbm.at[:, lanes], v.at[g], v_sem.at[g])

    def x_copy(g):
        rows = pl.ds(pl.multiple_of(g * DEPTH, DEPTH), DEPTH)
        return pltpu.make_async_copy(x.at[rows, :], x_hbm.at[rows, :], x_sem.at[g])

    for g in range(GROUPS):
        v_copy(g).start()
    my_zh, my_y, my_co = (lax.axis_index(a) for a in ROW_AXES)
    my_x = lax.axis_index("x")
    my_row = my_zh * 16 + my_y * 2 + my_co
    first = map_ref[0:1, :]
    second = map_ref[1:2, :]
    i = first - my_row * NCOLS
    j = (second * 2731) >> 16
    i_place = ((i & 3) ^ my_x) * 6 + (i >> 2)
    j_place = ((j & 1) ^ my_co) * 16 + ((j >> 1) & 7) * 2 + ((j >> 4) ^ my_zh)
    place = j_place * PAD + i_place
    weight = jnp.where(first == second, 0.5, 1.0)
    for start in range(0, places, 128):
        rows = lax.broadcasted_iota(jnp.int32, (128, slots), 0) + start
        onehot[start : start + 128, :] = jnp.where(rows == place, weight, 0.0).astype(
            jnp.bfloat16
        )

    @pl.loop(0, GROUPS)
    def _(g):
        v_copy(g).wait()
        for start in range(0, places, 256):
            dense[start : start + 256, :] = jnp.dot(
                onehot[start : start + 256, :], v[g], preferred_element_type=jnp.float32
            ).astype(jnp.bfloat16)
        for s in range(GROUP):
            parts = [
                dense[j * PAD : (j + 1) * PAD, s * TILE : (s + 1) * TILE] for j in range(NROWS)
            ]
            rows = pl.ds(pl.multiple_of(g * DEPTH + s * PAD, PAD), PAD)
            x[rows, :] = jnp.concatenate(parts, axis=1)
        x_copy(g).start()

    for g in range(GROUPS):
        x_copy(g).wait()


def place(tile_map, v_tiles):
    slots = v_tiles.shape[0]
    return pl.pallas_call(
        place_kernel,
        in_specs=[VMEM, HBM],
        out_specs=HBM,
        out_shape=jax.ShapeDtypeStruct((TALL, WIDE), jnp.bfloat16),
        scratch_shapes=[
            pltpu.VMEM((GROUPS, slots, LANES), jnp.bfloat16),
            pltpu.VMEM((TALL, WIDE), jnp.bfloat16),
            pltpu.VMEM((NROWS * PAD, slots), jnp.bfloat16),
            pltpu.VMEM((NROWS * PAD, LANES), jnp.bfloat16),
            pltpu.SemaphoreType.DMA((GROUPS,)),
            pltpu.SemaphoreType.DMA((GROUPS,)),
        ],
        compiler_params=params(60),
        cost_estimate=pl.CostEstimate(
            flops=2 * 1024 * 512 * 2304, bytes_accessed=8 * 2**20, transcendentals=0
        ),
        name="place",
    )(tile_map, v_tiles)


def copies_kernel(skip, *refs):
    *blocks, out = refs[skip:]
    for n in range(out.shape[0]):
        start = 0
        for block in blocks:
            out[n, start : start + block.shape[0], :] = block[...]
            start += block.shape[0]


def copies(count, after, *blocks):
    rows = sum(b.shape[0] for b in blocks)
    return pl.pallas_call(
        functools.partial(copies_kernel, len(after)),
        in_specs=[pl.BlockSpec(memory_space=pl.ANY)] * len(after) + [VMEM] * len(blocks),
        out_shape=jax.ShapeDtypeStruct((count, rows, PAIRS), blocks[0].dtype),
        compiler_params=params(4),
        name="copies",
    )(*after, *blocks)


def meet_kernel(after, x, block, out):
    out[...] = block[...]


def meet(after, x, block):
    return pl.pallas_call(
        meet_kernel,
        in_specs=[pl.BlockSpec(memory_space=pl.ANY), VMEM, VMEM],
        out_shape=jax.ShapeDtypeStruct(block.shape, block.dtype),
        compiler_params=params(16),
        name="meet",
    )(after, x, block)


def mirror_kernel(x, a0, a1, a2, a3, own_ref, other_ref, left, right, rows):
    quarters = (a0, a1, a2, a3)
    for h, wide in enumerate((left, right)):
        lanes = slice(h * 128, h * 128 + 128)
        for i in range(NCOLS):
            block = quarters[i // 6][i % 6, :, lanes]
            wide[pl.ds(i, TILE, stride=PAD), :] = block.astype(jnp.float32)
        for i in range(NCOLS, PAD):
            wide[pl.ds(i, TILE, stride=PAD), :] = jnp.zeros((TILE, 128), jnp.float32)
        rows[:, lanes] = wide[...].astype(jnp.bfloat16)
    for out, base in ((other_ref, HALF), (own_ref, 0)):
        for start in range(0, HALF, CHUNK):
            out[start : start + CHUNK, :] = lax.dot_general(
                x[:, base + start : base + start + CHUNK],
                rows[...],
                (((0,), (0,)), ((), ())),
                preferred_element_type=jnp.float32,
            )


def mirror(x, *quarters):
    half = jax.ShapeDtypeStruct((HALF, PAIRS), jnp.float32)
    return pl.pallas_call(
        mirror_kernel,
        out_shape=(half, half),
        scratch_shapes=[
            pltpu.VMEM((TALL, 128), jnp.float32),
            pltpu.VMEM((TALL, 128), jnp.float32),
            pltpu.VMEM((TALL, PAIRS), jnp.bfloat16),
        ],
        compiler_params=params(16),
        cost_estimate=pl.CostEstimate(
            flops=2 * TALL * WIDE * PAIRS, bytes_accessed=8 * 2**20, transcendentals=0
        ),
        name="mirror",
    )(x, *quarters)


def code(groups, out):
    row = lax.broadcasted_iota(jnp.int32, (EXTRA, PAIRS), 0)
    extra = jnp.zeros((EXTRA, PAIRS), jnp.int32)
    for n, block in enumerate(groups):
        top = jnp.max(jnp.abs(block), axis=0, keepdims=True)
        power = jnp.ceil(jnp.log2(jnp.maximum(top, 2.0**-100)))
        scaled = jnp.floor(block * jnp.exp2(15.0 - power) + 0.5)
        whole = jnp.clip(scaled, -32767.0, 32767.0).astype(jnp.int32)
        out[n * TILE : (n + 1) * TILE, :] = whole.astype(jnp.int16)
        extra = jnp.where(row == n, power.astype(jnp.int32), extra)
    out[len(groups) * TILE :, :] = extra.astype(jnp.int16)


def decode(coded, count):
    extra = coded[count * TILE :, :].astype(jnp.int32).astype(jnp.float32)
    step = jnp.exp2(extra - 15.0)
    return [
        coded[n * TILE : (n + 1) * TILE, :].astype(jnp.int32).astype(jnp.float32)
        * step[n : n + 1, :]
        for n in range(count)
    ]


def direct_kernel(x, own_ref, other_ref, o0, o1, o2, o3, left, right):
    for start in range(0, TALL, CHUNK):
        rows = slice(start, start + CHUNK)
        both = jnp.dot(
            x[rows, :HALF], own_ref[...], preferred_element_type=jnp.float32
        ) + jnp.dot(x[rows, HALF:], other_ref[...], preferred_element_type=jnp.float32)
        left[rows, :] = both[:, :128]
        right[rows, :] = both[:, 128:]

    def block(i):
        rows = pl.ds(i, TILE, stride=PAD)
        return jnp.concatenate([left[rows, :], right[rows, :]], axis=1)

    for q, out in ((1, o1), (2, o2), (3, o3)):
        code([block(q * 6 + n) for n in range(6)], out)
    for n in range(6):
        o0[n * TILE : (n + 1) * TILE, :] = block(n)


def direct(x, own, other):
    coded = jax.ShapeDtypeStruct((LINE + EXTRA, PAIRS), jnp.int16)
    return pl.pallas_call(
        direct_kernel,
        out_shape=(jax.ShapeDtypeStruct((LINE, PAIRS), jnp.float32),) + (coded,) * 3,
        scratch_shapes=[
            pltpu.VMEM((TALL, 128), jnp.float32),
            pltpu.VMEM((TALL, 128), jnp.float32),
        ],
        compiler_params=params(16),
        cost_estimate=pl.CostEstimate(
            flops=2 * TALL * WIDE * PAIRS, bytes_accessed=8 * 2**20, transcendentals=0
        ),
        name="direct",
    )(x, own, other)


def code_y_kernel(keep, got, out):
    @pl.loop(0, 8)
    def _(n):
        rows = pl.multiple_of(n * 2 * TILE, 2 * TILE)
        groups = [
            keep[pl.ds(rows + k * TILE, TILE), :] + got[pl.ds(rows + k * TILE, TILE), :]
            for k in range(2)
        ]
        code(groups, out.at[n])


def code_y(keep, got):
    return pl.pallas_call(
        code_y_kernel,
        out_shape=jax.ShapeDtypeStruct((8, 2 * TILE + EXTRA, PAIRS), jnp.int16),
        compiler_params=params(6),
        name="code_y",
    )(keep, got)


def sum_y_kernel(coded, near, send):
    totals = decode(coded.at[0], 2)
    for n in range(1, 8):
        totals = [a + b for a, b in zip(totals, decode(coded.at[n], 2))]
    near[...] = totals[0]
    code([totals[1]], send)


def sum_y(coded):
    return pl.pallas_call(
        sum_y_kernel,
        out_shape=(
            jax.ShapeDtypeStruct((TILE, PAIRS), jnp.float32),
            jax.ShapeDtypeStruct((TILE + EXTRA, PAIRS), jnp.int16),
        ),
        compiler_params=params(4),
        name="sum_y",
    )(coded)


def sum_x_kernel(keep, c1, c2, c3, out):
    parts = [decode(c, 6) for c in (c1, c2, c3)]
    for n in range(6):
        near = keep[n * TILE : (n + 1) * TILE, :]
        code([(near + parts[0][n]) + (parts[1][n] + parts[2][n])], out.at[n])


def sum_x(keep, *coded):
    return pl.pallas_call(
        sum_x_kernel,
        out_shape=jax.ShapeDtypeStruct((6, TILE + EXTRA, PAIRS), jnp.int16),
        compiler_params=params(4),
        name="sum_x",
    )(keep, *coded)


def end_kernel(residual, near, far, coded, out):
    line = [decode(coded.at[n], 1)[0] for n in range(6)]
    a = (line[0] + line[1]) + (line[2] + line[3])
    out[...] = (residual[...] + (near[...] + decode(far, 1)[0])) + (a + (line[4] + line[5]))


def end(residual, near, far, line):
    return pl.pallas_call(
        end_kernel,
        out_shape=jax.ShapeDtypeStruct((TILE, PAIRS), jnp.float32),
        compiler_params=params(4),
        name="end",
    )(residual, near, far, line)


SWAP = [(0, 1), (1, 0)]


def swap_x(block, k):
    return lax.ppermute(block, "x", [(i, i ^ k) for i in range(4)])


def trade(block, axis):
    return lax.all_to_all(block, axis, split_axis=0, concat_axis=0)


def per_device(amplitudes, residual_in, v_tiles, tile_map):
    far = lax.ppermute(amplitudes, "zh", SWAP)
    line = trade(copies(6, (), amplitudes), "zl")
    x = place(tile_map[0, 0].T, v_tiles[0, 0])
    x, far = lax.optimization_barrier((x, far))
    own = trade(copies(8, (), amplitudes, far), "y").reshape(HALF, PAIRS)
    quarters = [swap_x(line, k) for k in (1, 2, 3)]
    own, *quarters = lax.optimization_barrier((own, *quarters))
    other = lax.ppermute(own, "co", SWAP)
    near = meet(own, x, line)
    near, other = lax.optimization_barrier((near, other))
    keep, send = mirror(x, near, *quarters)
    got = lax.ppermute(send, "co", SWAP)
    parts = direct(x, own, other)
    got, *parts = lax.optimization_barrier((got, *parts))
    coded_y = code_y(keep, got)
    coded_y, *parts = lax.optimization_barrier((coded_y, *parts))
    row_parts = trade(coded_y, "y")

    col_line = sum_x(parts[0], *(swap_x(parts[k], k) for k in (1, 2, 3)))
    col_line = trade(col_line, "zl")

    row_near, row_send = sum_y(row_parts)
    row_far = lax.ppermute(row_send, "zh", SWAP)
    return end(residual_in, row_near, row_far, col_line)


def solution(mesh):
    fine = Mesh(mesh.devices.reshape(SIZES), AXES)
    return jax.shard_map(
        per_device,
        mesh=fine,
        in_specs=(
            P(AXES, None),
            P(AXES, None),
            P(ROW_AXES, COL_AXES, None, None),
            P(ROW_AXES, COL_AXES, None, None),
        ),
        out_specs=P(AXES, None),
        check_vma=False,
    )
```

```python
import functools

import jax
import jax.numpy as jnp
from jax import lax
from jax.experimental import pallas as pl
from jax.experimental.pallas import tpu as pltpu
from jax.sharding import Mesh, PartitionSpec as P

AXES = ("zh", "y", "co", "zl", "x")
SIZES = (2, 8, 2, 6, 4)
ROW_AXES = ("zh", "y", "co")
COL_AXES = ("zl", "x")
TILE = 48
PAIRS = 256
NCOLS = 24
NROWS = 32
PAD = 32
HALF = NROWS * TILE // 2
WIDE = NROWS * TILE
TALL = PAD * TILE
GROUP = 16
GROUPS = TILE // GROUP
LANES = GROUP * TILE
CHUNK = 256
DEPTH = GROUP * PAD
LINE = 6 * TILE
EXTRA = 16
HBM = pl.BlockSpec(memory_space=pltpu.HBM)
VMEM = pl.BlockSpec(memory_space=pltpu.VMEM)


def params(mib):
    return pltpu.CompilerParams(vmem_limit_bytes=mib * 2**20)


def place_kernel(map_ref, v_hbm, x_hbm, v, x, onehot, dense, v_sem, x_sem):
    slots = v_hbm.shape[0]
    places = NROWS * PAD

    def v_copy(g):
        lanes = pl.ds(pl.multiple_of(g * LANES, LANES), LANES)
        return pltpu.make_async_copy(v_hbm.at[:, lanes], v.at[g], v_sem.at[g])

    def x_copy(g):
        rows = pl.ds(pl.multiple_of(g * DEPTH, DEPTH), DEPTH)
        return pltpu.make_async_copy(x.at[rows, :], x_hbm.at[rows, :], x_sem.at[g])

    for g in range(GROUPS):
        v_copy(g).start()
    my_zh, my_y, my_co = (lax.axis_index(a) for a in ROW_AXES)
    my_x = lax.axis_index("x")
    my_row = my_zh * 16 + my_y * 2 + my_co
    first = map_ref[0:1, :]
    second = map_ref[1:2, :]
    i = first - my_row * NCOLS
    j = (second * 2731) >> 16
    i_place = ((i & 3) ^ my_x) * 6 + (i >> 2)
    j_place = ((j & 1) ^ my_co) * 16 + ((j >> 1) & 7) * 2 + ((j >> 4) ^ my_zh)
    place = j_place * PAD + i_place
    weight = jnp.where(first == second, 0.5, 1.0)
    for start in range(0, places, 128):
        rows = lax.broadcasted_iota(jnp.int32, (128, slots), 0) + start
        onehot[start : start + 128, :] = jnp.where(rows == place, weight, 0.0).astype(
            jnp.bfloat16
        )

    @pl.loop(0, GROUPS)
    def _(g):
        v_copy(g).wait()
        for start in range(0, places, 256):
            dense[start : start + 256, :] = jnp.dot(
                onehot[start : start + 256, :], v[g], preferred_element_type=jnp.float32
            ).astype(jnp.bfloat16)
        for s in range(GROUP):
            parts = [
                dense[j * PAD : (j + 1) * PAD, s * TILE : (s + 1) * TILE] for j in range(NROWS)
            ]
            rows = pl.ds(pl.multiple_of(g * DEPTH + s * PAD, PAD), PAD)
            x[rows, :] = jnp.concatenate(parts, axis=1)
        x_copy(g).start()

    for g in range(GROUPS):
        x_copy(g).wait()


def place(tile_map, v_tiles):
    slots = v_tiles.shape[0]
    return pl.pallas_call(
        place_kernel,
        in_specs=[VMEM, HBM],
        out_specs=HBM,
        out_shape=jax.ShapeDtypeStruct((TALL, WIDE), jnp.bfloat16),
        scratch_shapes=[
            pltpu.VMEM((GROUPS, slots, LANES), jnp.bfloat16),
            pltpu.VMEM((TALL, WIDE), jnp.bfloat16),
            pltpu.VMEM((NROWS * PAD, slots), jnp.bfloat16),
            pltpu.VMEM((NROWS * PAD, LANES), jnp.bfloat16),
            pltpu.SemaphoreType.DMA((GROUPS,)),
            pltpu.SemaphoreType.DMA((GROUPS,)),
        ],
        compiler_params=params(60),
        cost_estimate=pl.CostEstimate(
            flops=2 * 1024 * 512 * 2304, bytes_accessed=8 * 2**20, transcendentals=0
        ),
        name="place",
    )(tile_map, v_tiles)


def copies_kernel(skip, *refs):
    *blocks, out = refs[skip:]
    for n in range(out.shape[0]):
        start = 0
        for block in blocks:
            out[n, start : start + block.shape[0], :] = block[...]
            start += block.shape[0]


def copies(count, after, *blocks):
    rows = sum(b.shape[0] for b in blocks)
    return pl.pallas_call(
        functools.partial(copies_kernel, len(after)),
        in_specs=[pl.BlockSpec(memory_space=pl.ANY)] * len(after) + [VMEM] * len(blocks),
        out_shape=jax.ShapeDtypeStruct((count, rows, PAIRS), blocks[0].dtype),
        compiler_params=params(4),
        name="copies",
    )(*after, *blocks)


def meet_kernel(after, x, block, out):
    out[...] = block[...]


def meet(after, x, block):
    return pl.pallas_call(
        meet_kernel,
        in_specs=[pl.BlockSpec(memory_space=pl.ANY), VMEM, VMEM],
        out_shape=jax.ShapeDtypeStruct(block.shape, block.dtype),
        compiler_params=params(16),
        name="meet",
    )(after, x, block)


def mirror_kernel(x, a0, a1, a2, a3, own_ref, other_ref, left, right, rows):
    quarters = (a0, a1, a2, a3)
    for h, wide in enumerate((left, right)):
        lanes = slice(h * 128, h * 128 + 128)
        for i in range(NCOLS):
            block = quarters[i // 6][i % 6, :, lanes]
            wide[pl.ds(i, TILE, stride=PAD), :] = block.astype(jnp.float32)
        for i in range(NCOLS, PAD):
            wide[pl.ds(i, TILE, stride=PAD), :] = jnp.zeros((TILE, 128), jnp.float32)
        rows[:, lanes] = wide[...].astype(jnp.bfloat16)
    for out, base in ((other_ref, HALF), (own_ref, 0)):
        for start in range(0, HALF, CHUNK):
            out[start : start + CHUNK, :] = lax.dot_general(
                x[:, base + start : base + start + CHUNK],
                rows[...],
                (((0,), (0,)), ((), ())),
                preferred_element_type=jnp.float32,
            )


def mirror(x, *quarters):
    half = jax.ShapeDtypeStruct((HALF, PAIRS), jnp.float32)
    return pl.pallas_call(
        mirror_kernel,
        out_shape=(half, half),
        scratch_shapes=[
            pltpu.VMEM((TALL, 128), jnp.float32),
            pltpu.VMEM((TALL, 128), jnp.float32),
            pltpu.VMEM((TALL, PAIRS), jnp.bfloat16),
        ],
        compiler_params=params(16),
        cost_estimate=pl.CostEstimate(
            flops=2 * TALL * WIDE * PAIRS, bytes_accessed=8 * 2**20, transcendentals=0
        ),
        name="mirror",
    )(x, *quarters)


def code(groups, out):
    row = lax.broadcasted_iota(jnp.int32, (EXTRA, PAIRS), 0)
    extra = jnp.zeros((EXTRA, PAIRS), jnp.int32)
    for n, block in enumerate(groups):
        top = jnp.max(jnp.abs(block), axis=0, keepdims=True)
        power = jnp.ceil(jnp.log2(jnp.maximum(top, 2.0**-100)))
        scaled = jnp.floor(block * jnp.exp2(15.0 - power) + 0.5)
        whole = jnp.clip(scaled, -32767.0, 32767.0).astype(jnp.int32)
        out[n * TILE : (n + 1) * TILE, :] = whole.astype(jnp.int16)
        extra = jnp.where(row == n, power.astype(jnp.int32), extra)
    out[len(groups) * TILE :, :] = extra.astype(jnp.int16)


def decode(coded, count):
    extra = coded[count * TILE :, :].astype(jnp.int32).astype(jnp.float32)
    step = jnp.exp2(extra - 15.0)
    return [
        coded[n * TILE : (n + 1) * TILE, :].astype(jnp.int32).astype(jnp.float32)
        * step[n : n + 1, :]
        for n in range(count)
    ]


def direct_kernel(x, own_ref, other_ref, o0, o1, o2, o3, left, right):
    for start in range(0, TALL, CHUNK):
        rows = slice(start, start + CHUNK)
        both = jnp.dot(
            x[rows, :HALF], own_ref[...], preferred_element_type=jnp.float32
        ) + jnp.dot(x[rows, HALF:], other_ref[...], preferred_element_type=jnp.float32)
        left[rows, :] = both[:, :128]
        right[rows, :] = both[:, 128:]

    def block(i):
        rows = pl.ds(i, TILE, stride=PAD)
        return jnp.concatenate([left[rows, :], right[rows, :]], axis=1)

    for q, out in ((1, o1), (2, o2), (3, o3)):
        code([block(q * 6 + n) for n in range(6)], out)
    for n in range(6):
        o0[n * TILE : (n + 1) * TILE, :] = block(n)


def direct(x, own, other):
    coded = jax.ShapeDtypeStruct((LINE + EXTRA, PAIRS), jnp.int16)
    return pl.pallas_call(
        direct_kernel,
        out_shape=(jax.ShapeDtypeStruct((LINE, PAIRS), jnp.float32),) + (coded,) * 3,
        scratch_shapes=[
            pltpu.VMEM((TALL, 128), jnp.float32),
            pltpu.VMEM((TALL, 128), jnp.float32),
        ],
        compiler_params=params(16),
        cost_estimate=pl.CostEstimate(
            flops=2 * TALL * WIDE * PAIRS, bytes_accessed=8 * 2**20, transcendentals=0
        ),
        name="direct",
    )(x, own, other)


def code_y_kernel(keep, got, out):
    @pl.loop(0, 8)
    def _(n):
        rows = pl.multiple_of(n * 2 * TILE, 2 * TILE)
        groups = [
            keep[pl.ds(rows + k * TILE, TILE), :] + got[pl.ds(rows + k * TILE, TILE), :]
            for k in range(2)
        ]
        code(groups, out.at[n])


def code_y(keep, got):
    return pl.pallas_call(
        code_y_kernel,
        out_shape=jax.ShapeDtypeStruct((8, 2 * TILE + EXTRA, PAIRS), jnp.int16),
        compiler_params=params(6),
        name="code_y",
    )(keep, got)


def sum_y_kernel(coded, near, send):
    totals = decode(coded.at[0], 2)
    for n in range(1, 8):
        totals = [a + b for a, b in zip(totals, decode(coded.at[n], 2))]
    near[...] = totals[0]
    code([totals[1]], send)


def sum_y(coded):
    return pl.pallas_call(
        sum_y_kernel,
        out_shape=(
            jax.ShapeDtypeStruct((TILE, PAIRS), jnp.float32),
            jax.ShapeDtypeStruct((TILE + EXTRA, PAIRS), jnp.int16),
        ),
        compiler_params=params(4),
        name="sum_y",
    )(coded)


def sum_x_kernel(keep, c1, c2, c3, out):
    parts = [decode(c, 6) for c in (c1, c2, c3)]
    for n in range(6):
        near = keep[n * TILE : (n + 1) * TILE, :]
        code([(near + parts[0][n]) + (parts[1][n] + parts[2][n])], out.at[n])


def sum_x(keep, *coded):
    return pl.pallas_call(
        sum_x_kernel,
        out_shape=jax.ShapeDtypeStruct((6, TILE + EXTRA, PAIRS), jnp.int16),
        compiler_params=params(4),
        name="sum_x",
    )(keep, *coded)


def end_kernel(residual, near, far, coded, out):
    line = [decode(coded.at[n], 1)[0] for n in range(6)]
    a = (line[0] + line[1]) + (line[2] + line[3])
    out[...] = (residual[...] + (near[...] + decode(far, 1)[0])) + (a + (line[4] + line[5]))


def end(residual, near, far, line):
    return pl.pallas_call(
        end_kernel,
        out_shape=jax.ShapeDtypeStruct((TILE, PAIRS), jnp.float32),
        compiler_params=params(4),
        name="end",
    )(residual, near, far, line)


SWAP = [(0, 1), (1, 0)]


def swap_x(block, k):
    return lax.ppermute(block, "x", [(i, i ^ k) for i in range(4)])


def trade(block, axis):
    return lax.all_to_all(block, axis, split_axis=0, concat_axis=0)


def per_device(amplitudes, residual_in, v_tiles, tile_map):
    far = lax.ppermute(amplitudes, "zh", SWAP)
    line = trade(copies(6, (), amplitudes), "zl")
    x = place(tile_map[0, 0].T, v_tiles[0, 0])
    x, far = lax.optimization_barrier((x, far))
    own = trade(copies(8, (), amplitudes, far), "y").reshape(HALF, PAIRS)
    left, right = swap_x(line, 1), swap_x(line, 3)
    quarters = [left, swap_x(left, 3), right]
    own, *quarters = lax.optimization_barrier((own, *quarters))
    other = lax.ppermute(own, "co", SWAP)
    near = meet(own, x, line)
    near, other = lax.optimization_barrier((near, other))
    keep, send = mirror(x, near, *quarters)
    got = lax.ppermute(send, "co", SWAP)
    parts = direct(x, own, other)
    got, *parts = lax.optimization_barrier((got, *parts))
    coded_y = code_y(keep, got)
    coded_y, *parts = lax.optimization_barrier((coded_y, *parts))
    row_parts = trade(coded_y, "y")

    col_line = sum_x(parts[0], *(swap_x(parts[k], k) for k in (1, 2, 3)))
    col_line = trade(col_line, "zl")

    row_near, row_send = sum_y(row_parts)
    row_far = lax.ppermute(row_send, "zh", SWAP)
    return end(residual_in, row_near, row_far, col_line)


def solution(mesh):
    fine = Mesh(mesh.devices.reshape(SIZES), AXES)
    return jax.shard_map(
        per_device,
        mesh=fine,
        in_specs=(
            P(AXES, None),
            P(AXES, None),
            P(ROW_AXES, COL_AXES, None, None),
            P(ROW_AXES, COL_AXES, None, None),
        ),
        out_specs=P(AXES, None),
        check_vma=False,
    )
```

```python
import functools

import jax
import jax.numpy as jnp
from jax import lax
from jax.experimental import pallas as pl
from jax.experimental.pallas import tpu as pltpu
from jax.sharding import Mesh, PartitionSpec as P

AXES = ("zh", "y", "co", "zl", "x")
SIZES = (2, 8, 2, 6, 4)
ROW_AXES = ("zh", "y", "co")
COL_AXES = ("zl", "x")
TILE = 48
PAIRS = 256
NCOLS = 24
NROWS = 32
PAD = 32
HALF = NROWS * TILE // 2
WIDE = NROWS * TILE
TALL = PAD * TILE
GROUP = 16
GROUPS = TILE // GROUP
LANES = GROUP * TILE
CHUNK = 256
DEPTH = GROUP * PAD
LINE = 6 * TILE
EXTRA = 16
HBM = pl.BlockSpec(memory_space=pltpu.HBM)
VMEM = pl.BlockSpec(memory_space=pltpu.VMEM)


def params(mib):
    return pltpu.CompilerParams(vmem_limit_bytes=mib * 2**20)


def place_kernel(map_ref, v_hbm, x_hbm, v, x, onehot, dense, v_sem, x_sem):
    slots = v_hbm.shape[0]
    places = NROWS * PAD

    def v_copy(g):
        lanes = pl.ds(pl.multiple_of(g * LANES, LANES), LANES)
        return pltpu.make_async_copy(v_hbm.at[:, lanes], v.at[g], v_sem.at[g])

    def x_copy(g):
        rows = pl.ds(pl.multiple_of(g * DEPTH, DEPTH), DEPTH)
        return pltpu.make_async_copy(x.at[rows, :], x_hbm.at[rows, :], x_sem.at[g])

    for g in range(GROUPS):
        v_copy(g).start()
    my_zh, my_y, my_co = (lax.axis_index(a) for a in ROW_AXES)
    my_x = lax.axis_index("x")
    my_row = my_zh * 16 + my_y * 2 + my_co
    first = map_ref[0:1, :]
    second = map_ref[1:2, :]
    i = first - my_row * NCOLS
    j = (second * 2731) >> 16
    i_place = ((i & 3) ^ my_x) * 6 + (i >> 2)
    j_place = ((j & 1) ^ my_co) * 16 + ((j >> 1) & 7) * 2 + ((j >> 4) ^ my_zh)
    place = j_place * PAD + i_place
    weight = jnp.where(first == second, 0.5, 1.0)
    for start in range(0, places, 128):
        rows = lax.broadcasted_iota(jnp.int32, (128, slots), 0) + start
        onehot[start : start + 128, :] = jnp.where(rows == place, weight, 0.0).astype(
            jnp.bfloat16
        )

    @pl.loop(0, GROUPS)
    def _(g):
        v_copy(g).wait()
        for start in range(0, places, 256):
            dense[start : start + 256, :] = jnp.dot(
                onehot[start : start + 256, :], v[g], preferred_element_type=jnp.float32
            ).astype(jnp.bfloat16)
        for s in range(GROUP):
            parts = [
                dense[j * PAD : (j + 1) * PAD, s * TILE : (s + 1) * TILE] for j in range(NROWS)
            ]
            rows = pl.ds(pl.multiple_of(g * DEPTH + s * PAD, PAD), PAD)
            x[rows, :] = jnp.concatenate(parts, axis=1)
        x_copy(g).start()

    for g in range(GROUPS):
        x_copy(g).wait()


def place(tile_map, v_tiles):
    slots = v_tiles.shape[0]
    return pl.pallas_call(
        place_kernel,
        in_specs=[VMEM, HBM],
        out_specs=HBM,
        out_shape=jax.ShapeDtypeStruct((TALL, WIDE), jnp.bfloat16),
        scratch_shapes=[
            pltpu.VMEM((GROUPS, slots, LANES), jnp.bfloat16),
            pltpu.VMEM((TALL, WIDE), jnp.bfloat16),
            pltpu.VMEM((NROWS * PAD, slots), jnp.bfloat16),
            pltpu.VMEM((NROWS * PAD, LANES), jnp.bfloat16),
            pltpu.SemaphoreType.DMA((GROUPS,)),
            pltpu.SemaphoreType.DMA((GROUPS,)),
        ],
        compiler_params=params(60),
        cost_estimate=pl.CostEstimate(
            flops=2 * 1024 * 512 * 2304, bytes_accessed=8 * 2**20, transcendentals=0
        ),
        name="place",
    )(tile_map, v_tiles)


def copies_kernel(skip, *refs):
    *blocks, out = refs[skip:]
    for n in range(out.shape[0]):
        start = 0
        for block in blocks:
            out[n, start : start + block.shape[0], :] = block[...]
            start += block.shape[0]


def copies(count, after, *blocks):
    rows = sum(b.shape[0] for b in blocks)
    return pl.pallas_call(
        functools.partial(copies_kernel, len(after)),
        in_specs=[pl.BlockSpec(memory_space=pl.ANY)] * len(after) + [VMEM] * len(blocks),
        out_shape=jax.ShapeDtypeStruct((count, rows, PAIRS), blocks[0].dtype),
        compiler_params=params(4),
        name="copies",
    )(*after, *blocks)


def meet_kernel(after, x, block, out):
    out[...] = block[...]


def meet(after, x, block):
    return pl.pallas_call(
        meet_kernel,
        in_specs=[pl.BlockSpec(memory_space=pl.ANY), VMEM, VMEM],
        out_shape=jax.ShapeDtypeStruct(block.shape, block.dtype),
        compiler_params=params(16),
        name="meet",
    )(after, x, block)


def mirror_kernel(x, a0, a1, a2, a3, own_ref, other_ref, left, right, rows):
    quarters = (a0, a1, a2, a3)
    for h, wide in enumerate((left, right)):
        lanes = slice(h * 128, h * 128 + 128)
        for i in range(NCOLS):
            block = quarters[i // 6][i % 6, :, lanes]
            wide[pl.ds(i, TILE, stride=PAD), :] = block.astype(jnp.float32)
        for i in range(NCOLS, PAD):
            wide[pl.ds(i, TILE, stride=PAD), :] = jnp.zeros((TILE, 128), jnp.float32)
        rows[:, lanes] = wide[...].astype(jnp.bfloat16)
    for out, base in ((other_ref, HALF), (own_ref, 0)):
        for start in range(0, HALF, CHUNK):
            out[start : start + CHUNK, :] = lax.dot_general(
                x[:, base + start : base + start + CHUNK],
                rows[...],
                (((0,), (0,)), ((), ())),
                preferred_element_type=jnp.float32,
            )


def mirror(x, *quarters):
    half = jax.ShapeDtypeStruct((HALF, PAIRS), jnp.float32)
    return pl.pallas_call(
        mirror_kernel,
        out_shape=(half, half),
        scratch_shapes=[
            pltpu.VMEM((TALL, 128), jnp.float32),
            pltpu.VMEM((TALL, 128), jnp.float32),
            pltpu.VMEM((TALL, PAIRS), jnp.bfloat16),
        ],
        compiler_params=params(16),
        cost_estimate=pl.CostEstimate(
            flops=2 * TALL * WIDE * PAIRS, bytes_accessed=8 * 2**20, transcendentals=0
        ),
        name="mirror",
    )(x, *quarters)


def code(groups, out):
    row = lax.broadcasted_iota(jnp.int32, (EXTRA, PAIRS), 0)
    extra = jnp.zeros((EXTRA, PAIRS), jnp.int32)
    for n, block in enumerate(groups):
        top = jnp.max(jnp.abs(block), axis=0, keepdims=True)
        power = jnp.ceil(jnp.log2(jnp.maximum(top, 2.0**-100)))
        scaled = jnp.floor(block * jnp.exp2(15.0 - power) + 0.5)
        whole = jnp.clip(scaled, -32767.0, 32767.0).astype(jnp.int32)
        out[n * TILE : (n + 1) * TILE, :] = whole.astype(jnp.int16)
        extra = jnp.where(row == n, power.astype(jnp.int32), extra)
    out[len(groups) * TILE :, :] = extra.astype(jnp.int16)


def decode(coded, count):
    extra = coded[count * TILE :, :].astype(jnp.int32).astype(jnp.float32)
    step = jnp.exp2(extra - 15.0)
    return [
        coded[n * TILE : (n + 1) * TILE, :].astype(jnp.int32).astype(jnp.float32)
        * step[n : n + 1, :]
        for n in range(count)
    ]


def direct_kernel(x, own_ref, other_ref, o0, o1, o2, o3, left, right):
    for start in range(0, TALL, CHUNK):
        rows = slice(start, start + CHUNK)
        both = jnp.dot(
            x[rows, :HALF], own_ref[...], preferred_element_type=jnp.float32
        ) + jnp.dot(x[rows, HALF:], other_ref[...], preferred_element_type=jnp.float32)
        left[rows, :] = both[:, :128]
        right[rows, :] = both[:, 128:]

    def block(i):
        rows = pl.ds(i, TILE, stride=PAD)
        return jnp.concatenate([left[rows, :], right[rows, :]], axis=1)

    for q, out in ((1, o1), (2, o2), (3, o3)):
        code([block(q * 6 + n) for n in range(6)], out)
    for n in range(6):
        o0[n * TILE : (n + 1) * TILE, :] = block(n)


def direct(x, own, other):
    coded = jax.ShapeDtypeStruct((LINE + EXTRA, PAIRS), jnp.int16)
    return pl.pallas_call(
        direct_kernel,
        out_shape=(jax.ShapeDtypeStruct((LINE, PAIRS), jnp.float32),) + (coded,) * 3,
        scratch_shapes=[
            pltpu.VMEM((TALL, 128), jnp.float32),
            pltpu.VMEM((TALL, 128), jnp.float32),
        ],
        compiler_params=params(16),
        cost_estimate=pl.CostEstimate(
            flops=2 * TALL * WIDE * PAIRS, bytes_accessed=8 * 2**20, transcendentals=0
        ),
        name="direct",
    )(x, own, other)


def code_y_kernel(keep, got, out):
    @pl.loop(0, 8)
    def _(n):
        rows = pl.multiple_of(n * 2 * TILE, 2 * TILE)
        groups = [
            keep[pl.ds(rows + k * TILE, TILE), :] + got[pl.ds(rows + k * TILE, TILE), :]
            for k in range(2)
        ]
        code(groups, out.at[n])


def code_y(keep, got):
    return pl.pallas_call(
        code_y_kernel,
        out_shape=jax.ShapeDtypeStruct((8, 2 * TILE + EXTRA, PAIRS), jnp.int16),
        compiler_params=params(6),
        name="code_y",
    )(keep, got)


def sum_y_kernel(coded, near, send):
    totals = decode(coded.at[0], 2)
    for n in range(1, 8):
        totals = [a + b for a, b in zip(totals, decode(coded.at[n], 2))]
    near[...], send[...] = totals


def sum_y(coded):
    return pl.pallas_call(
        sum_y_kernel,
        out_shape=(jax.ShapeDtypeStruct((TILE, PAIRS), jnp.float32),) * 2,
        compiler_params=params(4),
        name="sum_y",
    )(coded)


def sum_x_kernel(keep, c1, c2, c3, out):
    parts = [decode(c, 6) for c in (c1, c2, c3)]
    for n in range(6):
        near = keep[n * TILE : (n + 1) * TILE, :]
        code([(near + parts[0][n]) + (parts[1][n] + parts[2][n])], out.at[n])


def sum_x(keep, *coded):
    return pl.pallas_call(
        sum_x_kernel,
        out_shape=jax.ShapeDtypeStruct((6, TILE + EXTRA, PAIRS), jnp.int16),
        compiler_params=params(4),
        name="sum_x",
    )(keep, *coded)


def end_kernel(residual, near, far, coded, out):
    line = [decode(coded.at[n], 1)[0] for n in range(6)]
    a = (line[0] + line[1]) + (line[2] + line[3])
    out[...] = (residual[...] + (near[...] + far[...])) + (a + (line[4] + line[5]))


def end(residual, near, far, line):
    return pl.pallas_call(
        end_kernel,
        out_shape=jax.ShapeDtypeStruct((TILE, PAIRS), jnp.float32),
        compiler_params=params(4),
        name="end",
    )(residual, near, far, line)


SWAP = [(0, 1), (1, 0)]


def swap_x(block, k):
    return lax.ppermute(block, "x", [(i, i ^ k) for i in range(4)])


def trade(block, axis):
    return lax.all_to_all(block, axis, split_axis=0, concat_axis=0)


def per_device(amplitudes, residual_in, v_tiles, tile_map):
    far = lax.ppermute(amplitudes, "zh", SWAP)
    line = trade(copies(6, (), amplitudes), "zl")
    x = place(tile_map[0, 0].T, v_tiles[0, 0])
    x, far = lax.optimization_barrier((x, far))
    own = trade(copies(8, (), amplitudes, far), "y").reshape(HALF, PAIRS)
    far_line, left, right = (swap_x(line, k) for k in (2, 1, 3))
    near = meet(own, x, line)
    quarters = [near, left, far_line, right]

    other = lax.ppermute(own, "co", SWAP)
    keep, send = mirror(x, *quarters)
    got = lax.ppermute(send, "co", SWAP)
    parts = direct(x, own, other)
    got, *parts = lax.optimization_barrier((got, *parts))
    coded_y = code_y(keep, got)
    coded_y, *parts = lax.optimization_barrier((coded_y, *parts))
    row_parts = trade(coded_y, "y")

    col_line = sum_x(parts[0], *(swap_x(parts[k], k) for k in (2, 1, 3)))
    col_line = trade(col_line, "zl")

    row_near, row_send = sum_y(row_parts)
    row_far = lax.ppermute(row_send, "zh", SWAP)
    return end(residual_in, row_near, row_far, col_line)


def solution(mesh):
    fine = Mesh(mesh.devices.reshape(SIZES), AXES)
    return jax.shard_map(
        per_device,
        mesh=fine,
        in_specs=(
            P(AXES, None),
            P(AXES, None),
            P(ROW_AXES, COL_AXES, None, None),
            P(ROW_AXES, COL_AXES, None, None),
        ),
        out_specs=P(AXES, None),
        check_vma=False,
    )
```

```python
import functools

import jax
import jax.numpy as jnp
from jax import lax
from jax.experimental import pallas as pl
from jax.experimental.pallas import tpu as pltpu
from jax.sharding import Mesh, PartitionSpec as P

AXES = ("zh", "y", "co", "zl", "x")
SIZES = (2, 8, 2, 6, 4)
ROW_AXES = ("zh", "y", "co")
COL_AXES = ("zl", "x")
TILE = 48
PAIRS = 256
NCOLS = 24
NROWS = 32
PAD = 32
HALF = NROWS * TILE // 2
WIDE = NROWS * TILE
TALL = PAD * TILE
GROUP = 16
GROUPS = TILE // GROUP
LANES = GROUP * TILE
CHUNK = 256
DEPTH = GROUP * PAD
LINE = 6 * TILE
EXTRA = 16
HBM = pl.BlockSpec(memory_space=pltpu.HBM)
VMEM = pl.BlockSpec(memory_space=pltpu.VMEM)


def params(mib):
    return pltpu.CompilerParams(vmem_limit_bytes=mib * 2**20)


def place_kernel(map_ref, v_hbm, x_hbm, v, x, onehot, dense, v_sem, x_sem):
    slots = v_hbm.shape[0]
    places = NROWS * PAD

    def v_copy(g):
        lanes = pl.ds(pl.multiple_of(g * LANES, LANES), LANES)
        return pltpu.make_async_copy(v_hbm.at[:, lanes], v.at[g], v_sem.at[g])

    def x_copy(g):
        rows = pl.ds(pl.multiple_of(g * DEPTH, DEPTH), DEPTH)
        return pltpu.make_async_copy(x.at[rows, :], x_hbm.at[rows, :], x_sem.at[g])

    for g in range(GROUPS):
        v_copy(g).start()
    my_zh, my_y, my_co = (lax.axis_index(a) for a in ROW_AXES)
    my_x = lax.axis_index("x")
    my_row = my_zh * 16 + my_y * 2 + my_co
    first = map_ref[0:1, :]
    second = map_ref[1:2, :]
    i = first - my_row * NCOLS
    j = (second * 2731) >> 16
    i_place = ((i & 3) ^ my_x) * 6 + (i >> 2)
    j_place = ((j & 1) ^ my_co) * 16 + ((j >> 1) & 7) * 2 + ((j >> 4) ^ my_zh)
    place = j_place * PAD + i_place
    weight = jnp.where(first == second, 0.5, 1.0)
    for start in range(0, places, 128):
        rows = lax.broadcasted_iota(jnp.int32, (128, slots), 0) + start
        onehot[start : start + 128, :] = jnp.where(rows == place, weight, 0.0).astype(
            jnp.bfloat16
        )

    @pl.loop(0, GROUPS)
    def _(g):
        v_copy(g).wait()
        for start in range(0, places, 256):
            dense[start : start + 256, :] = jnp.dot(
                onehot[start : start + 256, :], v[g], preferred_element_type=jnp.float32
            ).astype(jnp.bfloat16)
        for s in range(GROUP):
            parts = [
                dense[j * PAD : (j + 1) * PAD, s * TILE : (s + 1) * TILE] for j in range(NROWS)
            ]
            rows = pl.ds(pl.multiple_of(g * DEPTH + s * PAD, PAD), PAD)
            x[rows, :] = jnp.concatenate(parts, axis=1)
        x_copy(g).start()

    for g in range(GROUPS):
        x_copy(g).wait()


def place(tile_map, v_tiles):
    slots = v_tiles.shape[0]
    return pl.pallas_call(
        place_kernel,
        in_specs=[VMEM, HBM],
        out_specs=HBM,
        out_shape=jax.ShapeDtypeStruct((TALL, WIDE), jnp.bfloat16),
        scratch_shapes=[
            pltpu.VMEM((GROUPS, slots, LANES), jnp.bfloat16),
            pltpu.VMEM((TALL, WIDE), jnp.bfloat16),
            pltpu.VMEM((NROWS * PAD, slots), jnp.bfloat16),
            pltpu.VMEM((NROWS * PAD, LANES), jnp.bfloat16),
            pltpu.SemaphoreType.DMA((GROUPS,)),
            pltpu.SemaphoreType.DMA((GROUPS,)),
        ],
        compiler_params=params(60),
        cost_estimate=pl.CostEstimate(
            flops=2 * 1024 * 512 * 2304, bytes_accessed=8 * 2**20, transcendentals=0
        ),
        name="place",
    )(tile_map, v_tiles)


def copies_kernel(skip, *refs):
    *blocks, out = refs[skip:]
    for n in range(out.shape[0]):
        start = 0
        for block in blocks:
            out[n, start : start + block.shape[0], :] = block[...]
            start += block.shape[0]


def copies(count, after, *blocks):
    rows = sum(b.shape[0] for b in blocks)
    return pl.pallas_call(
        functools.partial(copies_kernel, len(after)),
        in_specs=[pl.BlockSpec(memory_space=pl.ANY)] * len(after) + [VMEM] * len(blocks),
        out_shape=jax.ShapeDtypeStruct((count, rows, PAIRS), blocks[0].dtype),
        compiler_params=params(4),
        name="copies",
    )(*after, *blocks)


def meet_kernel(after, x, block, out):
    out[...] = block[...]


def meet(after, x, block):
    return pl.pallas_call(
        meet_kernel,
        in_specs=[pl.BlockSpec(memory_space=pl.ANY), VMEM, VMEM],
        out_shape=jax.ShapeDtypeStruct(block.shape, block.dtype),
        compiler_params=params(16),
        name="meet",
    )(after, x, block)


def mirror_kernel(x, a0, a1, a2, a3, own_ref, other_ref, left, right, rows):
    quarters = (a0, a1, a2, a3)
    for h, wide in enumerate((left, right)):
        lanes = slice(h * 128, h * 128 + 128)
        for i in range(NCOLS):
            block = quarters[i // 6][i % 6, :, lanes]
            wide[pl.ds(i, TILE, stride=PAD), :] = block.astype(jnp.float32)
        for i in range(NCOLS, PAD):
            wide[pl.ds(i, TILE, stride=PAD), :] = jnp.zeros((TILE, 128), jnp.float32)
        rows[:, lanes] = wide[...].astype(jnp.bfloat16)
    for out, base in ((other_ref, HALF), (own_ref, 0)):
        for start in range(0, HALF, CHUNK):
            out[start : start + CHUNK, :] = lax.dot_general(
                x[:, base + start : base + start + CHUNK],
                rows[...],
                (((0,), (0,)), ((), ())),
                preferred_element_type=jnp.float32,
            )


def mirror(x, *quarters):
    half = jax.ShapeDtypeStruct((HALF, PAIRS), jnp.float32)
    return pl.pallas_call(
        mirror_kernel,
        out_shape=(half, half),
        scratch_shapes=[
            pltpu.VMEM((TALL, 128), jnp.float32),
            pltpu.VMEM((TALL, 128), jnp.float32),
            pltpu.VMEM((TALL, PAIRS), jnp.bfloat16),
        ],
        compiler_params=params(16),
        cost_estimate=pl.CostEstimate(
            flops=2 * TALL * WIDE * PAIRS, bytes_accessed=8 * 2**20, transcendentals=0
        ),
        name="mirror",
    )(x, *quarters)


def code(groups, out):
    row = lax.broadcasted_iota(jnp.int32, (EXTRA, PAIRS), 0)
    extra = jnp.zeros((EXTRA, PAIRS), jnp.int32)
    for n, block in enumerate(groups):
        top = jnp.max(jnp.abs(block), axis=0, keepdims=True)
        power = jnp.ceil(jnp.log2(jnp.maximum(top, 2.0**-100)))
        scaled = jnp.floor(block * jnp.exp2(15.0 - power) + 0.5)
        whole = jnp.clip(scaled, -32767.0, 32767.0).astype(jnp.int32)
        out[n * TILE : (n + 1) * TILE, :] = whole.astype(jnp.int16)
        extra = jnp.where(row == n, power.astype(jnp.int32), extra)
    out[len(groups) * TILE :, :] = extra.astype(jnp.int16)


def decode(coded, count):
    extra = coded[count * TILE :, :].astype(jnp.int32).astype(jnp.float32)
    step = jnp.exp2(extra - 15.0)
    return [
        coded[n * TILE : (n + 1) * TILE, :].astype(jnp.int32).astype(jnp.float32)
        * step[n : n + 1, :]
        for n in range(count)
    ]


def direct_kernel(x, own_ref, other_ref, o0, o1, o2, o3, left, right):
    for start in range(0, TALL, CHUNK):
        rows = slice(start, start + CHUNK)
        both = jnp.dot(
            x[rows, :HALF], own_ref[...], preferred_element_type=jnp.float32
        ) + jnp.dot(x[rows, HALF:], other_ref[...], preferred_element_type=jnp.float32)
        left[rows, :] = both[:, :128]
        right[rows, :] = both[:, 128:]

    def block(i):
        rows = pl.ds(i, TILE, stride=PAD)
        return jnp.concatenate([left[rows, :], right[rows, :]], axis=1)

    for q, out in ((1, o1), (2, o2), (3, o3)):
        code([block(q * 6 + n) for n in range(6)], out)
    for n in range(6):
        o0[n * TILE : (n + 1) * TILE, :] = block(n)


def direct(x, own, other):
    coded = jax.ShapeDtypeStruct((LINE + EXTRA, PAIRS), jnp.int16)
    return pl.pallas_call(
        direct_kernel,
        out_shape=(jax.ShapeDtypeStruct((LINE, PAIRS), jnp.float32),) + (coded,) * 3,
        scratch_shapes=[
            pltpu.VMEM((TALL, 128), jnp.float32),
            pltpu.VMEM((TALL, 128), jnp.float32),
        ],
        compiler_params=params(16),
        cost_estimate=pl.CostEstimate(
            flops=2 * TALL * WIDE * PAIRS, bytes_accessed=8 * 2**20, transcendentals=0
        ),
        name="direct",
    )(x, own, other)


def code_y_kernel(keep, got, out):
    @pl.loop(0, 8)
    def _(n):
        rows = pl.multiple_of(n * 2 * TILE, 2 * TILE)
        groups = [
            keep[pl.ds(rows + k * TILE, TILE), :] + got[pl.ds(rows + k * TILE, TILE), :]
            for k in range(2)
        ]
        code(groups, out.at[n])


def code_y(keep, got):
    return pl.pallas_call(
        code_y_kernel,
        out_shape=jax.ShapeDtypeStruct((8, 2 * TILE + EXTRA, PAIRS), jnp.int16),
        compiler_params=params(6),
        name="code_y",
    )(keep, got)


def sum_y_kernel(coded, near, send):
    totals = decode(coded.at[0], 2)
    for n in range(1, 8):
        totals = [a + b for a, b in zip(totals, decode(coded.at[n], 2))]
    near[...] = totals[0]
    code([totals[1]], send)


def sum_y(coded):
    return pl.pallas_call(
        sum_y_kernel,
        out_shape=(
            jax.ShapeDtypeStruct((TILE, PAIRS), jnp.float32),
            jax.ShapeDtypeStruct((TILE + EXTRA, PAIRS), jnp.int16),
        ),
        compiler_params=params(4),
        name="sum_y",
    )(coded)


def sum_x_kernel(keep, c1, c2, c3, out):
    parts = [decode(c, 6) for c in (c1, c2, c3)]
    for n in range(6):
        near = keep[n * TILE : (n + 1) * TILE, :]
        code([(near + parts[0][n]) + (parts[1][n] + parts[2][n])], out.at[n])


def sum_x(keep, *coded):
    return pl.pallas_call(
        sum_x_kernel,
        out_shape=jax.ShapeDtypeStruct((6, TILE + EXTRA, PAIRS), jnp.int16),
        compiler_params=params(4),
        name="sum_x",
    )(keep, *coded)


def end_kernel(residual, near, far, coded, out):
    line = [decode(coded.at[n], 1)[0] for n in range(6)]
    a = (line[0] + line[1]) + (line[2] + line[3])
    out[...] = (residual[...] + (near[...] + decode(far, 1)[0])) + (a + (line[4] + line[5]))


def end(residual, near, far, line):
    return pl.pallas_call(
        end_kernel,
        out_shape=jax.ShapeDtypeStruct((TILE, PAIRS), jnp.float32),
        compiler_params=params(4),
        name="end",
    )(residual, near, far, line)


SWAP = [(0, 1), (1, 0)]


def swap_x(block, k):
    return lax.ppermute(block, "x", [(i, i ^ k) for i in range(4)])


def trade(block, axis):
    return lax.all_to_all(block, axis, split_axis=0, concat_axis=0)


def per_device(amplitudes, residual_in, v_tiles, tile_map):
    far = lax.ppermute(amplitudes, "zh", SWAP)
    line = trade(copies(6, (), amplitudes), "zl")
    x = place(tile_map[0, 0].T, v_tiles[0, 0])
    x, far = lax.optimization_barrier((x, far))
    own = trade(copies(8, (), amplitudes, far), "y").reshape(HALF, PAIRS)
    quarters = [swap_x(line, k) for k in (1, 2, 3)]
    own, *quarters = lax.optimization_barrier((own, *quarters))
    other = lax.ppermute(own, "co", SWAP)
    near = meet(own, x, line)
    near, other = lax.optimization_barrier((near, other))
    keep, send = mirror(x, near, *quarters)
    got = lax.ppermute(send, "co", SWAP)
    parts = direct(x, own, other)
    got, *parts = lax.optimization_barrier((got, *parts))
    coded_y = code_y(keep, got)
    coded_y, *parts = lax.optimization_barrier((coded_y, *parts))
    row_parts = trade(coded_y, "y")

    col_line = sum_x(parts[0], *(swap_x(parts[k], k) for k in (2, 1, 3)))
    col_line = trade(col_line, "zl")

    row_near, row_send = sum_y(row_parts)
    row_far = lax.ppermute(row_send, "zh", SWAP)
    return end(residual_in, row_near, row_far, col_line)


def solution(mesh):
    fine = Mesh(mesh.devices.reshape(SIZES), AXES)
    return jax.shard_map(
        per_device,
        mesh=fine,
        in_specs=(
            P(AXES, None),
            P(AXES, None),
            P(ROW_AXES, COL_AXES, None, None),
            P(ROW_AXES, COL_AXES, None, None),
        ),
        out_specs=P(AXES, None),
        check_vma=False,
    )
```
